128 devices in a mesh: dp: 16 (over x, z_lo, core), tensor: 8 (over z_hi, y).
Axes of the slice: x: 4, y: 4, z: 4 (z_hi: 2, z_lo: 2; z = z_hi * 2 + z_lo), core: 2. Of those that a mesh axis runs over, the one named last changes fastest.
Arguments:
- tokens: bfloat16 [16384, 3072], P(('dp', 'tensor')), may hold values from -6 to 6
- cotangent: bfloat16 [16384, 3072], P(('dp', 'tensor')), may hold values from -6 to 6
- expert_ids: int32 [16384, 2], P(('dp', 'tensor')), may hold values from 0 to 7, as said below
- combine: float32 [16384], P(('dp', 'tensor')), may hold values from 0.2 to 1
- w_gate: bfloat16 [3072, 8192], P(None, 'tensor'), may hold values from -0.109375 to 0.109375
- w_up: bfloat16 [3072, 8192], P(None, 'tensor'), may hold values from -0.109375 to 0.109375
- w_down: bfloat16 [8192, 3072], P('tensor'), may hold values from -0.0625 to 0.0625
Outputs:
- expert_output: bfloat16 [16384, 3072], P(('dp', 'tensor'))
- token_grad: bfloat16 [16384, 3072], P(('dp', 'tensor'))
- gate_grad: bfloat16 [3072, 8192], P('dp', 'tensor')
- up_grad: bfloat16 [3072, 8192], P('dp', 'tensor')
- down_grad: bfloat16 [8192, 3072], P('tensor', 'dp')
The draws below stay inside these ranges and needn't reach their ends.
Inputs may be any that keep to these rules, and one draw needn't show every extreme that they name: `expert_ids`: each row names two different experts. Within each aligned block of 128 rows (the rows of one device) expert 0 is named by at most 48 rows, and in every draw all blocks of some group of 1024 rows name it exactly 48 times.
All inputs are finite; a program needn't handle non-finite values.
Results may differ from the reference program's by a relative error of at most 0.022.
Values may be sent and summed in bfloat16 or wider, within the bound.
No kernel may reach another device: no remote copies, remote signals or barrier semaphores. Data moves between devices by JAX's collectives and lax.ppermute only.
A program may use at most 192 MiB of HBM per device.

```python
import jax
import jax.numpy as jnp
from jax import lax

DW = 3072
FF_WIN = 8192
EXPERTS = 8
TOK_DEV = 128
DEV_CAP = 48
CAP = 384
TOKENS = 16384
N_DP = 16
N_TENSOR = 8


def draw_expert_ids(key, part):
    key = jax.random.fold_in(key, 7)
    blocks = TOKENS // TOK_DEV
    per_group = CAP // DEV_CAP
    key_list = jax.random.split(key, 6)
    divisor = 1 + jax.random.randint(key_list[0], (blocks,), 0, 8)
    counts = DEV_CAP // divisor
    full_group = jax.random.randint(key_list[1], (), 0, blocks // per_group)
    counts = jnp.where(jnp.arange(blocks) // per_group == full_group, DEV_CAP, counts)
    order_ranks = jax.vmap(lambda subkey: jax.random.permutation(subkey, TOK_DEV))(jax.random.split(key_list[2], blocks))
    chosen = order_ranks < counts[:, None]
    first_pick = 1 + jax.random.randint(key_list[3], (blocks, TOK_DEV), 0, EXPERTS - 1)
    step_offset = 1 + jax.random.randint(key_list[4], (blocks, TOK_DEV), 0, EXPERTS - 2)
    second_pick = 1 + (first_pick - 1 + step_offset) % (EXPERTS - 1)
    slot_side = jax.random.randint(key_list[5], (blocks, TOK_DEV), 0, 2)
    left_ids = jnp.where(chosen & (slot_side == 0), 0, first_pick)
    right_ids = jnp.where(chosen, jnp.where(slot_side == 0, first_pick, 0), second_pick)
    return jnp.stack([left_ids, right_ids], axis=-1).reshape(TOKENS, 2).astype(jnp.int32)


def levels(own_key, shape, shards, smallest, largest):
    level = 1.0
    for axis_at, parts in shards:
        steps = jax.random.uniform(jax.random.fold_in(jax.random.fold_in(own_key, 6), axis_at), (parts,), jnp.float32, smallest / len(shards), largest / len(shards))
        level = level * jnp.repeat(jnp.exp(steps), shape[axis_at] // parts).reshape((-1,) + (1,) * (len(shape) - 1 - axis_at))
    return level


def scatter_about(own_key, shape, scale, most, cuts=(), held_as=jnp.bfloat16):
    level = levels(own_key, shape, cuts, -0.22, 0.18) if cuts else 1.0
    result = jax.random.normal(own_key, shape, jnp.float32) * scale * level
    return jnp.minimum(jnp.maximum(result, -most), most).astype(held_as)


def setup_inputs(seed: int = 0) -> dict:
    key_of = jax.random.split(jax.random.key(seed), 8)
    return {
        "tokens": scatter_about(key_of[0], (TOKENS, DW), 1.0, 6.0, ((0, 128),)),
        "cotangent": scatter_about(key_of[1], (TOKENS, DW), 1.0, 6.0, ((0, 128),)),
        "expert_ids": draw_expert_ids(jax.random.fold_in(key_of[7], 71), 0),
        "combine": jnp.clip(0.2 + 0.8 * jax.random.uniform(key_of[3], (TOKENS,), jnp.float32) ** levels(key_of[3], (TOKENS,), ((0, 128),), -0.2, 0.2), 0.2, 1.0),
        "w_gate": scatter_about(key_of[4], (DW, FF_WIN), DW ** -0.5, 0.109375, ((1, 8),)),
        "w_up": scatter_about(key_of[5], (DW, FF_WIN), DW ** -0.5, 0.109375, ((1, 8),)),
        "w_down": scatter_about(key_of[6], (FF_WIN, DW), FF_WIN ** -0.5, 0.0625, ((0, 8),)),
    }


def reference(tokens, cotangent, expert_ids, combine, w_gate, w_up, w_down):
    group_size = TOK_DEV * N_TENSOR

    def one_group(totals, group_index):
        row_start = group_index * group_size
        x_group = lax.dynamic_slice_in_dim(tokens, row_start, group_size, 0)
        dy_group = lax.dynamic_slice_in_dim(cotangent, row_start, group_size, 0)
        ids_group = lax.dynamic_slice_in_dim(expert_ids, row_start, group_size, 0)
        weight = lax.dynamic_slice_in_dim(combine, row_start, group_size, 0)
        routed = jnp.any(ids_group == 0, axis=1)
        row_index = jnp.nonzero(routed, size=CAP, fill_value=0)[0].astype(jnp.int32)
        live_rows = (jnp.arange(CAP, dtype=jnp.int32) < jnp.sum(routed.astype(jnp.int32)))[:, None]
        d_all = (weight[:, None] * dy_group.astype(jnp.float32)).astype(jnp.bfloat16)
        x_rows = jnp.where(live_rows, x_group[row_index], jnp.zeros((), jnp.bfloat16))
        d_rows = jnp.where(live_rows, d_all[row_index], jnp.zeros((), jnp.bfloat16))
        gate_pre = jnp.dot(x_rows, w_gate, preferred_element_type=jnp.float32)
        up_pre = jnp.dot(x_rows, w_up, preferred_element_type=jnp.float32)
        sigmoid_gate = jax.nn.sigmoid(gate_pre)
        gate_act = gate_pre * sigmoid_gate
        hidden = (gate_act * up_pre).astype(jnp.bfloat16)
        out_rows = jnp.dot(hidden, w_down, preferred_element_type=jnp.float32)
        d_hidden = jnp.dot(d_rows, w_down.T, preferred_element_type=jnp.float32)
        d_up = (d_hidden * gate_act).astype(jnp.bfloat16)
        d_gate = (d_hidden * up_pre * sigmoid_gate * (1.0 + gate_pre * (1.0 - sigmoid_gate))).astype(jnp.bfloat16)
        back_rows = jnp.dot(d_gate, w_gate.T, preferred_element_type=jnp.float32) + jnp.dot(d_up, w_up.T, preferred_element_type=jnp.float32)
        zero_rows = jnp.zeros((group_size, DW), jnp.float32)
        placed_out = zero_rows.at[row_index].add(jnp.where(live_rows, out_rows, 0.0))
        placed_back = zero_rows.at[row_index].add(jnp.where(live_rows, back_rows, 0.0))
        y_group = (weight[:, None] * placed_out).astype(jnp.bfloat16)
        dx_group = placed_back.astype(jnp.bfloat16)
        term_gate = jnp.dot(x_rows.T, d_gate, preferred_element_type=jnp.float32)
        term_up = jnp.dot(x_rows.T, d_up, preferred_element_type=jnp.float32)
        term_down = jnp.dot(hidden.T, d_rows, preferred_element_type=jnp.float32)
        term_gate = lax.optimization_barrier(term_gate.astype(jnp.bfloat16)).astype(jnp.float32)
        term_up = lax.optimization_barrier(term_up.astype(jnp.bfloat16)).astype(jnp.float32)
        term_down = lax.optimization_barrier(term_down.astype(jnp.bfloat16)).astype(jnp.float32)
        totals = (totals[0] + term_gate, totals[1] + term_up, totals[2] + term_down)
        return totals, (y_group, dx_group)

    start_totals = (jnp.zeros((DW, FF_WIN), jnp.float32), jnp.zeros((DW, FF_WIN), jnp.float32), jnp.zeros((FF_WIN, DW), jnp.float32))
    totals, outputs = lax.scan(one_group, start_totals, jnp.arange(N_DP, dtype=jnp.int32))
    expert_output = outputs[0].reshape(TOKENS, DW)
    token_grad = outputs[1].reshape(TOKENS, DW)
    return (expert_output, token_grad, totals[0].astype(jnp.bfloat16), totals[1].astype(jnp.bfloat16), totals[2].astype(jnp.bfloat16))
```

```python
import functools
import itertools

import jax
import jax.numpy as jnp
from jax import lax
from jax.experimental import pallas as pl
from jax.experimental.pallas import tpu as pltpu
from jax.sharding import PartitionSpec as P

SLOTS = 48
ROWS = 384
DW = 3072
FF = 1024
HALF = 512
FEAT = 384
BF = jnp.bfloat16
F32 = jnp.float32
VMEM = 56 * 1024 * 1024

DIM = (4, 2, 2, 2, 4)


def linear(place):
    r = 0
    for q, n in zip(place, DIM):
        r = r * n + q % n
    return r


def shift(value, axis, by):
    pairs = []
    for place in itertools.product(*map(range, DIM)):
        to = list(place)
        to[axis] += by
        pairs.append((linear(place), linear(to)))
    return lax.ppermute(value, ("dp", "tensor"), pairs)


to_x = lambda v, by: shift(v, 0, by)
to_zlo = lambda v: shift(v, 1, 1)
to_core = lambda v: shift(v, 2, 1)
to_zhi = lambda v: shift(v, 3, 1)
to_y = lambda v, by: shift(v, 4, by)


def dot(a, b):
    return jnp.dot(a, b, preferred_element_type=F32)


def dot_t(a, b):
    return lax.dot_general(a, b, (((1,), (1,)), ((), ())), preferred_element_type=F32)


def t_dot(a, b):
    return lax.dot_general(a, b, (((0,), (0,)), ((), ())), preferred_element_type=F32)


def cost(flops, nbytes):
    return pl.CostEstimate(flops=int(flops), bytes_accessed=int(nbytes), transcendentals=0)


def params():
    return pltpu.CompilerParams(vmem_limit_bytes=VMEM)


def picks_of(ids, weight):
    n = ids.shape[1]
    chosen = (ids[0:1] == 0) | (ids[1:2] == 0)
    ones = jnp.where(chosen, 1.0, 0.0).astype(BF)
    before = lax.broadcasted_iota(jnp.int32, (n, n), 0) <= lax.broadcasted_iota(jnp.int32, (n, n), 1)
    place = dot(jnp.broadcast_to(ones, (8, n)), jnp.where(before, 1.0, 0.0).astype(BF))[0:1]
    place = place.astype(jnp.int32) - 1
    slot = lax.broadcasted_iota(jnp.int32, (SLOTS, n), 0)
    picks = jnp.where((place == slot) & chosen, 1.0, 0.0)
    return picks.astype(BF), jnp.sum(picks * weight, axis=1, keepdims=True)


def select_kernel(ids, weight, tokens, cotangent, x_sel, d_sel):
    picks, slot_weight = picks_of(ids[...], weight[...])
    x_sel[...] = dot(picks, tokens[...]).astype(BF)
    d_sel[...] = (dot(picks, cotangent[...]) * slot_weight).astype(BF)


def select(ids, weight, tokens, cotangent):
    out = jax.ShapeDtypeStruct((SLOTS, DW), BF)
    return pl.pallas_call(
        select_kernel,
        out_shape=(out, out),
        compiler_params=params(),
        cost_estimate=cost(4 * SLOTS * 128 * DW, 2.2e6),
    )(ids, weight, tokens, cotangent)


def place_kernel(scaled, ids, weight, own, got, out):
    picks, slot_weight = picks_of(ids[...], weight[...])
    total = own[...].astype(F32) + got[...].astype(F32)
    if scaled:
        total = total * slot_weight
    out[...] = t_dot(picks, total.astype(BF)).astype(BF)


def place(scaled, ids, weight, own, got):
    return pl.pallas_call(
        functools.partial(place_kernel, scaled),
        out_shape=jax.ShapeDtypeStruct((128, DW), BF),
        compiler_params=params(),
        cost_estimate=cost(2 * SLOTS * 128 * DW, 1.4e6),
    )(ids, weight, own, got)


def column(j, core):
    return ((1 - core[0]) * 2 + j) % 4


def chunk_spec():
    return pl.BlockSpec((SLOTS, DW), lambda j, core: (0, 0))


def natural_spec():
    return pl.BlockSpec((ROWS, 256), lambda j, core: (0, column(j, core)))


def sent_spec():
    return pl.BlockSpec((ROWS, 256), lambda j, core: (0, jnp.minimum(j, 1)))


def gate_kernel(core, *refs):
    chunks, (w_gate, w_up, rows, hidden, sent, act, slope) = refs[:8], refs[8:]
    j = pl.program_id(0)

    @pl.when(j == 0)
    def _():
        for k in range(8):
            rows[k * SLOTS : (k + 1) * SLOTS] = chunks[k][...]

    x = rows[...]
    gate = dot(x, w_gate[...])
    up = dot(x, w_up[...])
    s = jax.nn.sigmoid(gate)
    silu = gate * s
    act[...] = silu
    slope[...] = up * s * (1.0 + gate * (1.0 - s))
    h = (silu * up).astype(BF)
    hidden[...] = h

    @pl.when(j < 2)
    def _():
        sent[...] = h


def gate_up(core, chunks, w_gate, w_up):
    weight = pl.BlockSpec((DW, 256), lambda j, core: (0, column(j, core)))
    return pl.pallas_call(
        gate_kernel,
        grid_spec=pltpu.PrefetchScalarGridSpec(
            num_scalar_prefetch=1,
            grid=(4,),
            in_specs=[chunk_spec()] * 8 + [weight, weight],
            out_specs=[
                pl.BlockSpec((ROWS, DW), lambda j, core: (0, 0)),
                natural_spec(),
                sent_spec(),
                natural_spec(),
                natural_spec(),
            ],
        ),
        out_shape=(
            jax.ShapeDtypeStruct((ROWS, DW), BF),
            jax.ShapeDtypeStruct((ROWS, FF), BF),
            jax.ShapeDtypeStruct((ROWS, HALF), BF),
            jax.ShapeDtypeStruct((ROWS, FF), F32),
            jax.ShapeDtypeStruct((ROWS, FF), F32),
        ),
        compiler_params=params(),
        cost_estimate=cost(4 * ROWS * DW * FF, 21e6),
    )(core, *chunks, w_gate, w_up)


def back_kernel(core, *refs):
    chunks, (w_down, act, slope, rows, d_gate, d_up, sent) = refs[:8], refs[8:]
    j = pl.program_id(0)

    @pl.when(j == 0)
    def _():
        for k in range(8):
            rows[k * SLOTS : (k + 1) * SLOTS] = chunks[k][...]

    d_hidden = dot_t(rows[...], w_down[...])
    du = (d_hidden * act[...]).astype(BF)
    dg = (d_hidden * slope[...]).astype(BF)
    d_up[...] = du
    d_gate[...] = dg

    @pl.when(j < 2)
    def _():
        sent[0] = dg
        sent[1] = du


def back_hidden(core, chunks, w_down, act, slope):
    return pl.pallas_call(
        back_kernel,
        grid_spec=pltpu.PrefetchScalarGridSpec(
            num_scalar_prefetch=1,
            grid=(4,),
            in_specs=[chunk_spec()] * 8
            + [
                pl.BlockSpec((256, DW), lambda j, core: (column(j, core), 0)),
                natural_spec(),
                natural_spec(),
            ],
            out_specs=[
                pl.BlockSpec((ROWS, DW), lambda j, core: (0, 0)),
                natural_spec(),
                natural_spec(),
                pl.BlockSpec((2, ROWS, 256), lambda j, core: (0, 0, jnp.minimum(j, 1))),
            ],
        ),
        out_shape=(
            jax.ShapeDtypeStruct((ROWS, DW), BF),
            jax.ShapeDtypeStruct((ROWS, FF), BF),
            jax.ShapeDtypeStruct((ROWS, FF), BF),
            jax.ShapeDtypeStruct((2, ROWS, HALF), BF),
        ),
        compiler_params=params(),
        cost_estimate=cost(2 * ROWS * DW * FF, 16e6),
    )(core, *chunks, w_down, act, slope)


def out_kernel(hidden, w_down, out):
    out[...] = dot(hidden[...], w_down[...]).astype(BF)


def out_terms(hidden, w_down):
    return pl.pallas_call(
        out_kernel,
        grid=(4,),
        in_specs=[
            pl.BlockSpec((ROWS, FF), lambda j: (0, 0)),
            pl.BlockSpec((FF, 768), lambda j: (0, j)),
        ],
        out_specs=pl.BlockSpec((ROWS, 768), lambda j: (0, j)),
        out_shape=jax.ShapeDtypeStruct((ROWS, DW), BF),
        compiler_params=params(),
        cost_estimate=cost(2 * ROWS * DW * FF, 10e6),
    )(hidden, w_down)


def token_kernel(d_gate, d_up, w_gate, w_up, out):
    out[...] = (dot_t(d_gate[...], w_gate[...]) + dot_t(d_up[...], w_up[...])).astype(BF)


def token_terms(d_gate, d_up, w_gate, w_up):
    rows = pl.BlockSpec((ROWS, FF), lambda j: (0, 0))
    weight = pl.BlockSpec((768, FF), lambda j: (j, 0))
    return pl.pallas_call(
        token_kernel,
        grid=(4,),
        in_specs=[rows, rows, weight, weight],
        out_specs=pl.BlockSpec((ROWS, 768), lambda j: (0, j)),
        out_shape=jax.ShapeDtypeStruct((ROWS, DW), BF),
        compiler_params=params(),
        cost_estimate=cost(4 * ROWS * DW * FF, 18e6),
    )(d_gate, d_up, w_gate, w_up)


def both(own, other):
    return jnp.concatenate([own[...], other[...]], axis=0)


def feature_spec():
    return pl.BlockSpec((ROWS, FEAT), lambda j, core, order: (0, order[j]))


def half_spec():
    return pl.BlockSpec((ROWS, HALF), lambda j, core, order: (0, core[0]))


def other_spec():
    return pl.BlockSpec((ROWS, HALF), lambda j, core, order: (0, 0))


def grads_kernel(core, order, x_own, x_other, g_own, g_other, u_own, u_other, gate, up):
    x = both(x_own, x_other)
    gate[0] = t_dot(x, both(g_own, g_other)).astype(BF)
    up[0] = t_dot(x, both(u_own, u_other)).astype(BF)


def gate_up_grads(core, order, x_own, x_other, d_gate, d_up, got):
    g_other = pl.BlockSpec((None, ROWS, HALF), lambda j, core, order: (0, 0, 0))
    u_other = pl.BlockSpec((None, ROWS, HALF), lambda j, core, order: (1, 0, 0))
    out = pl.BlockSpec((1, FEAT, HALF), lambda j, core, order: (j, 0, 0))
    shape = jax.ShapeDtypeStruct((8, FEAT, HALF), BF)
    return pl.pallas_call(
        grads_kernel,
        grid_spec=pltpu.PrefetchScalarGridSpec(
            num_scalar_prefetch=2,
            grid=(8,),
            in_specs=[
                feature_spec(),
                feature_spec(),
                half_spec(),
                g_other,
                half_spec(),
                u_other,
            ],
            out_specs=[out, out],
        ),
        out_shape=(shape, shape),
        compiler_params=params(),
        cost_estimate=cost(4 * ROWS * DW * FF, 13e6),
    )(core, order, x_own, x_other, d_gate, got, d_up, got)


def down_kernel(core, order, d_own, d_other, h_own, h_other, out, h_turned):
    @pl.when(pl.program_id(0) == 0)
    def _():
        h_turned[...] = both(h_own, h_other).T

    out[0] = dot(h_turned[...], both(d_own, d_other)).astype(BF)


def down_grads(core, order, d_own, d_other, hidden, got):
    return pl.pallas_call(
        down_kernel,
        grid_spec=pltpu.PrefetchScalarGridSpec(
            num_scalar_prefetch=2,
            grid=(8,),
            in_specs=[feature_spec(), feature_spec(), half_spec(), other_spec()],
            out_specs=pl.BlockSpec((1, HALF, FEAT), lambda j, core, order: (j, 0, 0)),
            scratch_shapes=[pltpu.VMEM((HALF, 2 * ROWS), BF)],
        ),
        out_shape=jax.ShapeDtypeStruct((8, HALF, FEAT), BF),
        compiler_params=params(),
        cost_estimate=cost(2 * ROWS * DW * FF, 9e6),
    )(core, order, d_own, d_other, hidden, got)


def add(*terms):
    return sum(t.astype(F32) for t in terms).astype(BF)


def gather_rows(own):
    up0 = to_y(own, -1)
    down0 = to_y(own, 1)
    other = to_zhi(own)
    far0 = to_y(up0, -1)
    up1 = to_y(other, -1)
    down1 = to_y(other, 1)
    far1 = to_y(down1, 1)
    return [far0, far1, up0, up1, down0, down1, own, other]


def sum_rows(terms):
    t = [terms[k * SLOTS : (k + 1) * SLOTS] for k in range(8)]
    a = to_y(t[0], 1)
    b = to_y(t[1], -1)
    above = to_y(jnp.concatenate([add(t[2], a), t[3]], axis=0), 1)
    below = to_y(jnp.concatenate([t[4], add(t[5], b)], axis=0), -1)
    own = add(t[6], above[:SLOTS], below[:SLOTS])
    other = add(t[7], above[SLOTS:], below[SLOTS:])
    return own, to_zhi(other)


def sum_x(far, far_other, near, back, own):
    a = to_x(far, 1)
    b = to_x(far_other, -1)
    above = to_x(jnp.concatenate([add(near[0], a), near[1]], axis=0), 1)
    below = to_x(jnp.concatenate([back[0], add(back[1], b)], axis=0), -1)
    return add(own, above, below)


def sum_x_first(m):
    s = sum_x(m[0:1], m[1:2], (m[2:3], m[3:4]), (m[4:5], m[5:6]), m[6:8])
    return add(s[0], to_zlo(s[1]))


def sum_zlo_first(m):
    got = to_zlo(m[0:4])
    s = add(m[4:8], got)
    h = s.shape[1] // 2
    parts = lambda k: (s[k, :h], s[k, h:])
    return sum_x(*parts(0), parts(1), parts(2), s[3])


def local(tokens, cotangent, expert_ids, combine, w_gate, w_up, w_down):
    dp = lax.axis_index("dp")
    x, zlo, c = dp // 4, (dp // 2) % 2, dp % 2
    core = c.astype(jnp.int32).reshape(1)

    def order_of(steps):
        return jnp.stack([((x + dx) % 4) * 2 + (zlo + dz) % 2 for dx, dz in steps]).astype(jnp.int32)

    x_first = order_of([(dx, dz) for dx in (2, 1, 3, 0) for dz in (0, 1)])
    ids, weight = expert_ids.T, combine.reshape(1, -1)

    x_sel, d_sel = select(ids, weight, tokens, cotangent)
    x_chunks = gather_rows(x_sel)
    d_chunks = gather_rows(d_sel)
    x_rows, hidden, hidden_sent, act, slope = gate_up(core, x_chunks, w_gate, w_up)
    x_other = to_core(x_rows)
    hidden_got = to_core(hidden_sent)
    out = out_terms(hidden, w_down)
    d_rows, d_gate, d_up, d_sent = back_hidden(core, d_chunks, w_down, act, slope)
    d_got = to_core(d_sent)
    d_other = to_core(d_rows)
    gate, up = gate_up_grads(core, x_first, x_rows, x_other, d_gate, d_up, d_got)
    zlo_first = order_of([(dx, dz) for dz in (1, 0) for dx in (2, 1, 3, 0)])
    down = down_grads(core, zlo_first, d_rows, d_other, hidden, hidden_got)
    back = token_terms(d_gate, d_up, w_gate, w_up)

    gate_sum = sum_x_first(gate)
    up_sum = sum_x_first(up)
    down_sum = sum_zlo_first(down)
    out_own, out_got = sum_rows(out)
    back_own, back_got = sum_rows(back)
    expert_output = place(True, ids, weight, out_own, out_got)
    token_grad = place(False, ids, weight, back_own, back_got)

    def join(s, axis, other_axis):
        low, high = jnp.split(s, 2, axis=axis)
        keep = jnp.where(c == 0, low, high)
        got = to_core(jnp.where(c == 0, high, low))
        first, second = jnp.where(c == 0, keep, got), jnp.where(c == 0, got, keep)
        return jnp.concatenate([first, second], axis=other_axis)

    return (expert_output, token_grad, join(gate_sum, 0, 1), join(up_sum, 0, 1), join(down_sum, 1, 0))


def solution(mesh):
    placed = (
        P(("dp", "tensor"), None),
        P(("dp", "tensor"), None),
        P(("dp", "tensor"), None),
        P(("dp", "tensor")),
        P(None, "tensor"),
        P(None, "tensor"),
        P("tensor", None),
    )
    return jax.shard_map(
        local,
        mesh=mesh,
        in_specs=placed,
        out_specs=(
            P(("dp", "tensor"), None),
            P(("dp", "tensor"), None),
            P("dp", "tensor"),
            P("dp", "tensor"),
            P("tensor", "dp"),
        ),
        check_vma=False,
    )
```

```python
import functools
import itertools
import math

import jax
import jax.numpy as jnp
from jax import lax
from jax.experimental import pallas as pl
from jax.experimental.pallas import tpu as pltpu
from jax.sharding import PartitionSpec as P

SLOTS = 48
ROWS = 384
DW = 3072
FF = 1024
HALF = 512
FEAT = 384
BF = jnp.bfloat16
F32 = jnp.float32
VMEM = 10 * 1024 * 1024

IN_VMEM = pl.BlockSpec(memory_space=pltpu.VMEM)
IN_SMEM = pl.BlockSpec(memory_space=pltpu.SMEM)
IN_HBM = pl.BlockSpec(memory_space=pltpu.HBM)

DIM = (4, 2, 2, 2, 4)


def linear(place):
    r = 0
    for q, n in zip(place, DIM):
        r = r * n + q % n
    return r


def shift(value, axis, by):
    pairs = []
    for place in itertools.product(*map(range, DIM)):
        to = list(place)
        to[axis] += by
        pairs.append((linear(place), linear(to)))
    return lax.ppermute(value, ("dp", "tensor"), pairs)


to_x = lambda v, by: shift(v, 0, by)
to_zlo = lambda v: shift(v, 1, 1)
to_core = lambda v: shift(v, 2, 1)
to_zhi = lambda v: shift(v, 3, 1)
to_y = lambda v, by: shift(v, 4, by)


def dot(a, b):
    return jnp.dot(a, b, preferred_element_type=F32)


def dot_t(a, b):
    return lax.dot_general(a, b, (((1,), (1,)), ((), ())), preferred_element_type=F32)


def t_dot(a, b):
    return lax.dot_general(a, b, (((0,), (0,)), ((), ())), preferred_element_type=F32)


def cost(flops, nbytes):
    return pl.CostEstimate(flops=int(flops / 10), bytes_accessed=int(nbytes / 10), transcendentals=0)


def params():
    return pltpu.CompilerParams(vmem_limit_bytes=VMEM)


def after(value, *others):
    return lax.optimization_barrier((value, *others))[0]


def picks_of(ids, weight):
    n = ids.shape[1]
    chosen = (ids[0:1] == 0) | (ids[1:2] == 0)
    ones = jnp.where(chosen, 1.0, 0.0).astype(BF)
    before = lax.broadcasted_iota(jnp.int32, (n, n), 0) <= lax.broadcasted_iota(jnp.int32, (n, n), 1)
    place = dot(jnp.broadcast_to(ones, (8, n)), jnp.where(before, 1.0, 0.0).astype(BF))[0:1]
    place = place.astype(jnp.int32) - 1
    slot = lax.broadcasted_iota(jnp.int32, (SLOTS, n), 0)
    picks = jnp.where((place == slot) & chosen, 1.0, 0.0)
    return picks.astype(BF), jnp.sum(picks * weight, axis=1, keepdims=True)


def select_kernel(scaled, ids, weight, values, out, ids_here, weight_here, values_here, sems):
    copies = [
        pltpu.make_async_copy(ids, ids_here, sems.at[0]),
        pltpu.make_async_copy(weight, weight_here, sems.at[1]),
        pltpu.make_async_copy(values, values_here, sems.at[2]),
    ]
    for copy in copies:
        copy.start()
    for copy in copies:
        copy.wait()
    picks, slot_weight = picks_of(ids_here[...], weight_here[...])
    rows = dot(picks, values_here[...])
    if scaled:
        rows = rows * slot_weight
    out[...] = rows.astype(BF)


def in_hbm(array):
    return pltpu.with_memory_space_constraint(array, pltpu.HBM)


def select(scaled, ids, weight, values):
    arrays = (ids, weight, values)
    return pl.pallas_call(
        functools.partial(select_kernel, scaled),
        in_specs=[IN_HBM] * 3,
        out_specs=IN_VMEM,
        out_shape=pltpu.VMEM((SLOTS, DW), BF),
        scratch_shapes=[pltpu.VMEM(a.shape, a.dtype) for a in arrays]
        + [pltpu.SemaphoreType.DMA((3,))],
        compiler_params=params(),
        cost_estimate=cost(2 * SLOTS * 128 * DW, 1.1e6),
    )(*map(in_hbm, arrays))


def place_kernel(ids, weight, kept, got, output, token_grad):
    picks, slot_weight = picks_of(ids[...], weight[...])
    out = kept[0].astype(F32) + got[0].astype(F32)
    output[...] = t_dot(picks, (out * slot_weight).astype(BF)).astype(BF)
    back = kept[1].astype(F32) + got[1].astype(F32)
    token_grad[...] = t_dot(picks, back.astype(BF)).astype(BF)


def place_rows(ids, weight, kept, got):
    return pl.pallas_call(
        place_kernel,
        in_specs=[IN_VMEM] * 4,
        out_specs=[IN_VMEM] * 2,
        out_shape=[jax.ShapeDtypeStruct((128, DW), BF)] * 2,
        compiler_params=params(),
        cost_estimate=cost(4 * SLOTS * 128 * DW, 2.8e6),
    )(ids, weight, kept, got)


def call(kernel, scalars, arrays, shapes, flops, scratch=()):
    shapes = [s if isinstance(s[0], tuple) else (s, BF) for s in shapes]
    size = sum(a.size for a in arrays) + sum(math.prod(s) for s, _ in shapes)
    return pl.pallas_call(
        kernel,
        in_specs=[IN_SMEM] * len(scalars) + [IN_VMEM] * len(arrays),
        out_specs=[IN_VMEM] * len(shapes),
        out_shape=[pltpu.VMEM(s, t) for s, t in shapes],
        scratch_shapes=list(scratch),
        compiler_params=params(),
        cost_estimate=cost(flops, size),
    )(*scalars, *arrays)


def stage_kernel(n, *refs):
    sems = refs[-1]
    copies = [pltpu.make_async_copy(refs[i], refs[n + 1 + i], sems.at[i]) for i in range(n)]
    for copy in copies:
        copy.start()
    for copy in copies:
        copy.wait()


def stage(arrays, earlier):
    n = len(arrays)
    return pl.pallas_call(
        functools.partial(stage_kernel, n),
        in_specs=[IN_HBM] * n + [pl.BlockSpec(memory_space=pl.ANY)],
        out_specs=[IN_VMEM] * n,
        out_shape=[pltpu.VMEM(a.shape, a.dtype) for a in arrays],
        scratch_shapes=[pltpu.SemaphoreType.DMA((n,))],
        compiler_params=params(),
        cost_estimate=cost(1, 4 * sum(a.size for a in arrays)),
    )(*map(in_hbm, arrays), earlier)


def half(h):
    return pl.ds(pl.multiple_of(h * HALF, HALF), HALF)


def gather(chunks, rows):
    for k in range(8):
        rows[k * SLOTS : (k + 1) * SLOTS] = chunks[k][...]


def gate_kernel(core, *refs):
    chunks, (w_gate, w_up, rows, hidden, sent, act, slope) = refs[:8], refs[8:]
    gather(chunks, rows)
    for h in range(2):
        at = slice(h * HALF, (h + 1) * HALF)
        gate = dot(rows[...], w_gate[:, at])
        up = dot(rows[...], w_up[:, at])
        s = jax.nn.sigmoid(gate)
        silu = gate * s
        act[:, at] = silu
        slope[:, at] = up * s * (1.0 + gate * (1.0 - s))
        hidden[:, at] = (silu * up).astype(BF)
    sent[...] = hidden[:, half(1 - core[0])]


def gate_up(core, chunks, w_gate, w_up):
    shapes = [(ROWS, DW), (ROWS, FF), (ROWS, HALF), ((ROWS, FF), F32), ((ROWS, FF), F32)]
    return call(gate_kernel, [core], [*chunks, w_gate, w_up], shapes, 4 * ROWS * DW * FF)


def back_kernel(core, *refs):
    chunks, (w_down, act, slope, rows, d_gate, d_up, sent) = refs[:8], refs[8:]
    gather(chunks, rows)
    for h in range(2):
        at = slice(h * HALF, (h + 1) * HALF)
        d_hidden = dot_t(rows[...], w_down[at, :])
        d_up[:, at] = (d_hidden * act[:, at]).astype(BF)
        d_gate[:, at] = (d_hidden * slope[:, at]).astype(BF)
    sent[0] = d_gate[:, half(1 - core[0])]
    sent[1] = d_up[:, half(1 - core[0])]


def back_hidden(core, chunks, w_down, act, slope):
    shapes = [(ROWS, DW), (ROWS, FF), (ROWS, FF), (2, ROWS, HALF)]
    return call(back_kernel, [core], [*chunks, w_down, act, slope], shapes, 2 * ROWS * DW * FF)


def out_kernel(hidden, w_down, out):
    for j in range(0, DW, 768):
        at = slice(j, j + 768)
        out[:, at] = dot(hidden[...], w_down[:, at]).astype(BF)


def out_terms(hidden, w_down):
    return call(out_kernel, [], [hidden, w_down], [(ROWS, DW)], 2 * ROWS * DW * FF)[0]


def token_kernel(d_gate, d_up, w_gate, w_up, out, far_a, far_b, above, below, own):
    targets = [far_a, far_b] + [t.at[dz] for t in (above, below, own) for dz in range(2)]
    for j in range(0, DW, 768):
        at = slice(j, j + 768)
        back = dot_t(d_gate[...], w_gate[at, :]) + dot_t(d_up[...], w_up[at, :])
        for k, target in enumerate(targets):
            rows = slice(k * SLOTS, (k + 1) * SLOTS)
            target[0, :, at] = out[rows, at]
            target[1, :, at] = back[rows].astype(BF)


def row_terms(d_gate, d_up, w_gate, w_up, out):
    shapes = [(2, SLOTS, DW)] * 2 + [(2, 2, SLOTS, DW)] * 3
    return call(token_kernel, [], [d_gate, d_up, w_gate, w_up, out], shapes, 4 * ROWS * DW * FF)


def both(own, other):
    return jnp.concatenate([own, other], axis=0)


def features(place, dx):
    at = ((place[2] + dx) % 4) * (2 * FEAT)
    return pl.ds(pl.multiple_of(at, 2 * FEAT), 2 * FEAT)


def store_pair(place, first, second, low, high):
    @pl.when(place[1] == 0)
    def _():
        first[...] = low
        second[...] = high

    @pl.when(place[1] == 1)
    def _():
        first[...] = high
        second[...] = low


def grads_kernel(steps, place, x_own, x_other, d_gate, d_up, got, *outs):
    mine = half(place[0])
    for k, dx in enumerate(steps):
        at = features(place, dx)
        x = both(x_own[:, at], x_other[:, at])
        for m, terms in enumerate((d_gate, d_up)):
            result = t_dot(x, both(terms[:, mine], got[m])).astype(BF)
            low, high = outs[2 * k].at[m], outs[2 * k + 1].at[m]
            store_pair(place, low, high, result[:FEAT], result[FEAT:])


def gate_up_grads(place, steps, x_own, x_other, d_gate, d_up, got):
    return call(
        functools.partial(grads_kernel, steps),
        [place],
        [x_own, x_other, d_gate, d_up, got],
        [(2, FEAT, HALF)] * (2 * len(steps)),
        len(steps) * ROWS * DW * FF,
    )


def down_kernel(place, d_own, d_other, hidden, got, kept, sent):
    h = both(hidden[:, half(place[0])], got[...])
    for k, dx in enumerate((2, 1, 3, 0)):
        at = features(place, dx)
        result = t_dot(both(d_own[:, at], d_other[:, at]), h).astype(BF)
        store_pair(place, kept.at[k], sent.at[k], result[:FEAT], result[FEAT:])


def down_grads(place, d_own, d_other, hidden, got):
    shapes = [(4, FEAT, HALF)] * 2
    return call(down_kernel, [place], [d_own, d_other, hidden, got], shapes, 2 * ROWS * DW * FF)


def add(*terms):
    return sum(t[...].astype(F32) for t in terms).astype(BF)


def add_pairs_kernel(n, *refs):
    for k in range(n):
        refs[2 * n + k][...] = add(refs[2 * k], refs[2 * k + 1])


def add_pairs(*terms):
    n = len(terms) // 2
    shapes = [t.shape for t in terms[::2]]
    kernel = functools.partial(add_pairs_kernel, n)
    return call(kernel, [], terms, shapes, sum(math.prod(s) for s in shapes))


def add_all_kernel(*refs):
    refs[-1][...] = add(*refs[:-1])


def add_all(*terms):
    return call(add_all_kernel, [], terms, [terms[0].shape], 2 * terms[0].size)[0]


def add_into_kernel(above, got_a, below, got_b, new_above, new_below):
    new_above[0] = add(above.at[0], got_a)
    new_above[1] = above[1]
    new_below[0] = below[0]
    new_below[1] = add(below.at[1], got_b)


def add_into(above, got_a, below, got_b):
    return call(add_into_kernel, [], [above, got_a, below, got_b], [above.shape] * 2, above.size)


def add_three_kernel(own, above, below, kept, sent):
    kept[...] = add(own.at[0], above.at[0], below.at[0])
    sent[...] = add(own.at[1], above.at[1], below.at[1])


def add_three(own, above, below):
    return call(add_three_kernel, [], [own, above, below], [own.shape[1:]] * 2, 2 * own.size)


def halves_kernel(place, *refs):
    *terms, mine, theirs = refs
    total = add(*terms)
    low, high = total[:, : FEAT // 2], total[:, FEAT // 2 :]

    @pl.when(place[0] == 0)
    def _():
        mine[...] = low
        theirs[...] = high

    @pl.when(place[0] == 1)
    def _():
        mine[...] = high
        theirs[...] = low


def halves(place, *terms):
    n = terms[0].shape[0]
    return call(halves_kernel, [place], terms, [(n, FEAT // 2, HALF)] * 2, 2 * terms[0].size)


def join_kernel(place, mine, got, *outs):
    for k, out in enumerate(outs):

        @pl.when(place[0] == 0)
        def _():
            out[:, :HALF] = mine[k]
            out[:, HALF:] = got[k]

        @pl.when(place[0] == 1)
        def _():
            out[:, :HALF] = got[k]
            out[:, HALF:] = mine[k]


def join(place, mine, got):
    n = mine.shape[0]
    return pl.pallas_call(
        join_kernel,
        in_specs=[IN_SMEM, IN_VMEM, IN_VMEM],
        out_specs=[IN_VMEM] * n,
        out_shape=[jax.ShapeDtypeStruct((FEAT // 2, FF), BF)] * n,
        compiler_params=params(),
        cost_estimate=cost(mine.size, 8 * mine.size),
    )(place, mine, got)


def cut_kernel(kept, got, far_a, far_b, above, below, own):
    n = FEAT // 2
    far = add(kept.at[0], got.at[0])
    far_a[...] = far[:n]
    far_b[...] = far[n:]
    for k, out in enumerate((above, below)):
        total = add(kept.at[1 + k], got.at[1 + k])
        out[0] = total[:n]
        out[1] = total[n:]
    own[0] = add(kept.at[3], got.at[3])


def cut(kept, got):
    n = FEAT // 2
    shapes = [(n, HALF)] * 2 + [(2, n, HALF)] * 2 + [(1, FEAT, HALF)]
    return call(cut_kernel, [], [kept, got], shapes, kept.size)


def local(tokens, cotangent, expert_ids, combine, w_gate, w_up, w_down):
    dp = lax.axis_index("dp")
    place = jnp.stack([dp % 2, (dp // 2) % 2, dp // 4]).astype(jnp.int32)
    ids, weight = expert_ids.T, combine.reshape(1, -1)

    x_sel = select(False, ids, weight, tokens)
    x_1, x_up0, x_down0, x_far0 = to_zhi(x_sel), to_y(x_sel, -1), to_y(x_sel, 1), to_y(x_sel, 2)
    d_sel = select(True, ids, weight, after(cotangent, x_sel))
    d_1 = to_zhi(d_sel)
    w_gate, w_up = stage([w_gate, w_up], d_sel)
    x_up1, x_down1, x_far1 = to_zhi(x_up0), to_zhi(x_down0), to_y(x_1, 2)
    d_now = after(d_sel, x_far0)
    d_up0, d_down0 = to_y(d_now, -1), to_y(d_now, 1)
    w_down = stage([w_down], w_gate)[0]
    d_far0 = to_y(after(d_sel, x_far1), 2)
    d_1_now = after(d_1, x_up1, x_down1)
    d_up1, d_down1 = to_y(d_1_now, -1), to_y(d_1_now, 1)
    x_chunks = [x_far0, x_far1, x_up0, x_up1, x_down0, x_down1, x_sel, x_1]
    x_rows, hidden, hidden_sent, act, slope = gate_up(place, x_chunks, w_gate, w_up)
    d_far1 = to_zhi(d_far0)
    x_other = to_core(x_rows)
    hidden_got = to_core(hidden_sent)
    out = out_terms(hidden, w_down)
    d_chunks = [d_far0, d_far1, d_up0, d_up1, d_down0, d_down1, after(d_sel, out), d_1]
    d_rows, d_gate, d_up, d_sent = back_hidden(place, d_chunks, w_down, act, slope)
    d_got = to_core(d_sent)
    d_other = to_core(d_rows)
    row_far_a, row_far_b, row_above, row_below, row_own = row_terms(d_gate, d_up, w_gate, w_up, out)

    far_a, far_b = gate_up_grads(place, (2,), x_rows, x_other, after(d_gate, row_own), d_up, d_got)
    row_far_a, row_far_b = to_y(row_far_a, 1), to_y(row_far_b, -1)
    d_ready = after(d_rows, far_a)
    far_a, far_b = to_x(far_a, 1), to_x(far_b, -1)
    down_kept, down_sent = down_grads(place, d_ready, d_other, hidden, hidden_got)
    down_got = to_zlo(down_sent)
    above0, above1, below0, below1, own0, own1 = gate_up_grads(
        place, (1, 3, 0), x_rows, x_other, after(d_gate, down_kept), d_up, d_got
    )
    row_above, row_below = add_into(after(row_above, own0), row_far_a, row_below, row_far_b)
    row_above, row_below = to_y(row_above, 1), to_y(row_below, -1)
    above0, below1 = add_pairs(above0, far_a, below1, far_b)
    above1, below1 = to_x(above1, 1), to_x(below1, -1)
    above0, below0 = to_x(above0, 1), to_x(below0, -1)
    row_kept, row_sent = add_three(row_own, row_above, row_below)
    row_got = to_zhi(row_sent)
    sum1 = to_zlo(add_all(own1, above1, below1))
    expert_output, token_grad = place_rows(ids, weight, row_kept, row_got)
    far_a, far_b, above, below, down_own = cut(down_kept, down_got)
    far_a, far_b = to_x(far_a, 1), to_x(far_b, -1)
    mine, theirs = halves(place, own0, above0, below0, sum1)
    gate_grad, up_grad = join(place, mine, to_core(theirs))
    above, below = add_into(above, far_a, below, far_b)
    whole = lambda v: v.reshape(1, FEAT, HALF)
    above, below = whole(to_x(above, 1)), whole(to_x(below, -1))
    mine, theirs = halves(place, down_own, above, below)
    (down_grad,) = join(place, mine, to_core(theirs))
    return (expert_output, token_grad, gate_grad, up_grad, down_grad.T)


def solution(mesh):
    placed = (
        P(("dp", "tensor"), None),
        P(("dp", "tensor"), None),
        P(("dp", "tensor"), None),
        P(("dp", "tensor")),
        P(None, "tensor"),
        P(None, "tensor"),
        P("tensor", None),
    )
    return jax.shard_map(
        local,
        mesh=mesh,
        in_specs=placed,
        out_specs=(
            P(("dp", "tensor"), None),
            P(("dp", "tensor"), None),
            P("dp", "tensor"),
            P("dp", "tensor"),
            P("tensor", "dp"),
        ),
        check_vma=False,
    )
```

```python
import functools
import itertools
import math

import jax
import jax.numpy as jnp
from jax import lax
from jax.experimental import pallas as pl
from jax.experimental.pallas import tpu as pltpu
from jax.sharding import PartitionSpec as P

SLOTS = 48
ROWS = 384
DW = 3072
FF = 1024
HALF = 512
FEAT = 384
BF = jnp.bfloat16
F32 = jnp.float32
VMEM = 10 * 1024 * 1024
COST = 1000

IN_VMEM = pl.BlockSpec(memory_space=pltpu.VMEM)
IN_SMEM = pl.BlockSpec(memory_space=pltpu.SMEM)
IN_HBM = pl.BlockSpec(memory_space=pltpu.HBM)

DIM = (4, 2, 2, 2, 4)


def linear(place):
    r = 0
    for q, n in zip(place, DIM):
        r = r * n + q % n
    return r


def shift(value, axis, by):
    pairs = []
    for place in itertools.product(*map(range, DIM)):
        to = list(place)
        to[axis] += by
        pairs.append((linear(place), linear(to)))
    return lax.ppermute(value, ("dp", "tensor"), pairs)


to_x = lambda v, by: shift(v, 0, by)
to_zlo = lambda v: shift(v, 1, 1)
to_core = lambda v: shift(v, 2, 1)
to_zhi = lambda v: shift(v, 3, 1)
to_y = lambda v, by: shift(v, 4, by)


def dot(a, b):
    return jnp.dot(a, b, preferred_element_type=F32)


def dot_t(a, b):
    return lax.dot_general(a, b, (((1,), (1,)), ((), ())), preferred_element_type=F32)


def t_dot(a, b):
    return lax.dot_general(a, b, (((0,), (0,)), ((), ())), preferred_element_type=F32)


def cost(flops, nbytes):
    return pl.CostEstimate(flops=int(flops / COST), bytes_accessed=int(nbytes / COST), transcendentals=0)


def params():
    return pltpu.CompilerParams(vmem_limit_bytes=VMEM)


def after(value, *others):
    return lax.optimization_barrier((value, *others))[0]


def picks_of(ids, weight):
    n = ids.shape[1]
    chosen = (ids[0:1] == 0) | (ids[1:2] == 0)
    ones = jnp.where(chosen, 1.0, 0.0).astype(BF)
    before = lax.broadcasted_iota(jnp.int32, (n, n), 0) <= lax.broadcasted_iota(jnp.int32, (n, n), 1)
    place = dot(jnp.broadcast_to(ones, (8, n)), jnp.where(before, 1.0, 0.0).astype(BF))[0:1]
    place = place.astype(jnp.int32) - 1
    slot = lax.broadcasted_iota(jnp.int32, (SLOTS, n), 0)
    picks = jnp.where((place == slot) & chosen, 1.0, 0.0)
    return picks.astype(BF), jnp.sum(picks * weight, axis=1, keepdims=True)


def select_kernel(ids, weight, x, d, out, ids_here, weight_here, x_here, d_here, sems):
    copies = [
        pltpu.make_async_copy(far, near, sems.at[k])
        for k, (far, near) in enumerate(
            ((ids, ids_here), (weight, weight_here), (x, x_here), (d, d_here))
        )
    ]
    for copy in copies:
        copy.start()
    copies[0].wait()
    copies[1].wait()
    picks, slot_weight = picks_of(ids_here[...], weight_here[...])
    copies[2].wait()
    out[0] = dot(picks, x_here[...]).astype(BF)
    copies[3].wait()
    out[1] = (dot(picks, d_here[...]) * slot_weight).astype(BF)


def in_hbm(array):
    return pltpu.with_memory_space_constraint(array, pltpu.HBM)


def select(*arrays):
    return pl.pallas_call(
        select_kernel,
        in_specs=[IN_HBM] * 4,
        out_specs=IN_VMEM,
        out_shape=pltpu.VMEM((2, SLOTS, DW), BF),
        scratch_shapes=[pltpu.VMEM(a.shape, a.dtype) for a in arrays]
        + [pltpu.SemaphoreType.DMA((4,))],
        compiler_params=params(),
        cost_estimate=cost(4 * SLOTS * 128 * DW, 2.2e6),
    )(*map(in_hbm, arrays))


def place_kernel(ids, weight, kept, got, output, token_grad):
    picks, slot_weight = picks_of(ids[...], weight[...])
    out = kept[0].astype(F32) + got[0].astype(F32)
    output[...] = t_dot(picks, (out * slot_weight).astype(BF)).astype(BF)
    back = kept[1].astype(F32) + got[1].astype(F32)
    token_grad[...] = t_dot(picks, back.astype(BF)).astype(BF)


def place_rows(ids, weight, kept, got):
    return pl.pallas_call(
        place_kernel,
        in_specs=[IN_VMEM] * 4,
        out_specs=[IN_VMEM] * 2,
        out_shape=[jax.ShapeDtypeStruct((128, DW), BF)] * 2,
        compiler_params=params(),
        cost_estimate=cost(4 * SLOTS * 128 * DW, 2.8e6),
    )(ids, weight, kept, got)


IN_ANY = pl.BlockSpec(memory_space=pl.ANY)


def without(first, count, kernel):
    def run(*refs):
        kernel(*refs[:first], *refs[first + count :])

    return run


def call(kernel, scalars, arrays, shapes, flops, earlier=(), hbm=(), scratch=()):
    shapes = [s if isinstance(s[0], tuple) else (s, BF) for s in shapes]
    size = sum(a.size for a in arrays) + sum(math.prod(s) for s, _ in shapes)
    inputs = len(scalars) + len(arrays) + len(hbm)
    return pl.pallas_call(
        without(inputs, len(earlier), kernel),
        in_specs=[IN_SMEM] * len(scalars)
        + [IN_VMEM] * len(arrays)
        + [IN_HBM] * len(hbm)
        + [IN_ANY] * len(earlier),
        out_specs=[IN_VMEM] * len(shapes),
        out_shape=[pltpu.VMEM(s, t) for s, t in shapes],
        scratch_shapes=list(scratch),
        compiler_params=params(),
        cost_estimate=cost(flops, size),
    )(*scalars, *arrays, *map(in_hbm, hbm), *earlier)


def stage_kernel(n, *refs):
    sems = refs[-1]
    copies = [pltpu.make_async_copy(refs[i], refs[n + i], sems.at[i]) for i in range(n)]
    for copy in copies:
        copy.start()
    for copy in copies:
        copy.wait()


def stage(arrays, *earlier):
    return call(
        functools.partial(stage_kernel, len(arrays)),
        [],
        [],
        [a.shape for a in arrays],
        1,
        earlier,
        hbm=arrays,
        scratch=[pltpu.SemaphoreType.DMA((len(arrays),))],
    )


def half(h):
    return pl.ds(pl.multiple_of(h * HALF, HALF), HALF)


def gather(which, chunks, rows):
    for k, chunk in enumerate(chunks):
        rows[k * SLOTS : (k + 1) * SLOTS] = chunk[...] if len(chunk.shape) == 2 else chunk[which]


def gather_kernel(*refs):
    gather(0, refs[:8], refs[8])


def gather_rows(chunks, *earlier):
    return call(gather_kernel, [], chunks, [(ROWS, DW)], 1, earlier)[0]


def split_kernel(a, b, x, d):
    x[...] = a[0]
    d[...] = b[1]


def split(a, b):
    return call(split_kernel, [], [a, b], [(SLOTS, DW)] * 2, 1)


def gate_kernel(core, rows, w_gate, w_up, hidden, sent, act, slope):
    for h in range(2):
        at = slice(h * HALF, (h + 1) * HALF)
        gate = dot(rows[...], w_gate[:, at])
        up = dot(rows[...], w_up[:, at])
        s = jax.nn.sigmoid(gate)
        silu = gate * s
        act[:, at] = silu
        slope[:, at] = up * s * (1.0 + gate * (1.0 - s))
        hidden[:, at] = (silu * up).astype(BF)
    sent[...] = hidden[:, half(1 - core[0])]


def gate_up(core, rows, w_gate, w_up):
    shapes = [(ROWS, FF), (ROWS, HALF), ((ROWS, FF), F32), ((ROWS, FF), F32)]
    return call(gate_kernel, [core], [rows, w_gate, w_up], shapes, 4 * ROWS * DW * FF)


def back_kernel(core, *refs):
    chunks, (w_down, act, slope, rows, d_gate, d_up, sent) = refs[:8], refs[8:]
    gather(1, chunks, rows)
    for h in range(2):
        at = slice(h * HALF, (h + 1) * HALF)
        d_hidden = dot_t(rows[...], w_down[at, :])
        d_up[:, at] = (d_hidden * act[:, at]).astype(BF)
        d_gate[:, at] = (d_hidden * slope[:, at]).astype(BF)
    sent[0] = d_gate[:, half(1 - core[0])]
    sent[1] = d_up[:, half(1 - core[0])]


def back_hidden(core, chunks, w_down, act, slope):
    shapes = [(ROWS, DW), (ROWS, FF), (ROWS, FF), (2, ROWS, HALF)]
    return call(back_kernel, [core], [*chunks, w_down, act, slope], shapes, 2 * ROWS * DW * FF)


def out_kernel(hidden, w_down, out):
    for j in range(0, DW, 768):
        at = slice(j, j + 768)
        out[:, at] = dot(hidden[...], w_down[:, at]).astype(BF)


def out_terms(hidden, w_down, *earlier):
    return call(out_kernel, [], [hidden, w_down], [(ROWS, DW)], 2 * ROWS * DW * FF, earlier)[0]


def token_kernel(d_gate, d_up, w_gate, w_up, out, far_a, far_b, above, below, own):
    targets = [far_a, far_b] + [t.at[dz] for t in (above, below, own) for dz in range(2)]
    for j in range(0, DW, 768):
        at = slice(j, j + 768)
        back = dot_t(d_gate[...], w_gate[at, :]) + dot_t(d_up[...], w_up[at, :])
        for k, target in enumerate(targets):
            rows = slice(k * SLOTS, (k + 1) * SLOTS)
            target[0, :, at] = out[rows, at]
            target[1, :, at] = back[rows].astype(BF)


def row_terms(d_gate, d_up, w_gate, w_up, out, *earlier):
    shapes = [(2, SLOTS, DW)] * 2 + [(2, 2, SLOTS, DW)] * 3
    arrays = [d_gate, d_up, w_gate, w_up, out]
    return call(token_kernel, [], arrays, shapes, 4 * ROWS * DW * FF, earlier)


def both(own, other):
    return jnp.concatenate([own, other], axis=0)


def features(place, dx):
    at = ((place[2] + dx) % 4) * (2 * FEAT)
    return pl.ds(pl.multiple_of(at, 2 * FEAT), 2 * FEAT)


def store_pair(place, first, second, low, high):
    @pl.when(place[1] == 0)
    def _():
        first[...] = low
        second[...] = high

    @pl.when(place[1] == 1)
    def _():
        first[...] = high
        second[...] = low


def grads_kernel(pairs, place, x_own, x_other, d_gate, d_up, got, *outs):
    mine = half(place[0])
    terms = [both(t[:, mine], got[m]) for m, t in enumerate((d_gate, d_up))]
    outs = list(outs)
    for dx, dz in pairs:
        if dz is None:
            at = features(place, dx)
        else:
            at = ((place[2] + dx) % 4) * (2 * FEAT) + ((place[1] + dz) % 2) * FEAT
            at = pl.ds(pl.multiple_of(at, FEAT), FEAT)
        x = both(x_own[:, at], x_other[:, at])
        here = [outs.pop(0) for _ in range(2 if dz is None else 1)]
        for m in range(2):
            result = t_dot(x, terms[m]).astype(BF)
            if dz is None:
                store_pair(place, here[0].at[m], here[1].at[m], result[:FEAT], result[FEAT:])
            else:
                here[0][m] = result


def gate_up_grads(place, pairs, x_own, x_other, d_gate, d_up, got, *earlier):
    n = sum(2 if dz is None else 1 for _, dz in pairs)
    return call(
        functools.partial(grads_kernel, pairs),
        [place],
        [x_own, x_other, d_gate, d_up, got],
        [(2, FEAT, HALF)] * n,
        n * ROWS * DW * FF / 2,
        earlier,
    )


def down_kernel(place, d_own, d_other, hidden, got, kept, sent):
    h = both(hidden[:, half(place[0])], got[...])
    for k, dx in enumerate((2, 1, 3, 0)):
        at = features(place, dx)
        result = t_dot(both(d_own[:, at], d_other[:, at]), h).astype(BF)
        store_pair(place, kept.at[k], sent.at[k], result[:FEAT], result[FEAT:])


def down_grads(place, d_own, d_other, hidden, got, *earlier):
    shapes = [(4, FEAT, HALF)] * 2
    return call(down_kernel, [place], [d_own, d_other, hidden, got], shapes, 2 * ROWS * DW * FF, earlier)


def add(*terms):
    return sum(t[...].astype(F32) for t in terms).astype(BF)


def add_pairs_kernel(n, *refs):
    for k in range(n):
        refs[2 * n + k][...] = add(refs[2 * k], refs[2 * k + 1])


def add_pairs(*terms):
    n = len(terms) // 2
    shapes = [t.shape for t in terms[::2]]
    flops = sum(math.prod(s) for s in shapes)
    return call(functools.partial(add_pairs_kernel, n), [], terms, shapes, flops)


def add_all_kernel(*refs):
    refs[-1][...] = add(*refs[:-1])


def add_all(*terms):
    return call(add_all_kernel, [], terms, [terms[0].shape], 2 * terms[0].size)[0]


def add_into_kernel(above, got_a, below, got_b, new_above, new_below):
    new_above[0] = add(above.at[0], got_a)
    new_above[1] = above[1]
    new_below[0] = below[0]
    new_below[1] = add(below.at[1], got_b)


def add_into(above, got_a, below, got_b, *earlier):
    return call(
        add_into_kernel, [], [above, got_a, below, got_b], [above.shape] * 2, above.size, earlier
    )


def add_three_kernel(own, above, below, kept, sent):
    kept[...] = add(own.at[0], above.at[0], below.at[0])
    sent[...] = add(own.at[1], above.at[1], below.at[1])


def add_three(own, above, below):
    return call(add_three_kernel, [], [own, above, below], [own.shape[1:]] * 2, 2 * own.size)


def halves_kernel(place, *refs):
    *terms, mine, theirs = refs
    total = add(*terms)
    low, high = total[:, : FEAT // 2], total[:, FEAT // 2 :]

    @pl.when(place[0] == 0)
    def _():
        mine[...] = low
        theirs[...] = high

    @pl.when(place[0] == 1)
    def _():
        mine[...] = high
        theirs[...] = low


def halves(place, *terms):
    n = terms[0].shape[0]
    return call(halves_kernel, [place], terms, [(n, FEAT // 2, HALF)] * 2, 2 * terms[0].size)


def join_kernel(place, mine, got, *outs):
    for k, out in enumerate(outs):

        @pl.when(place[0] == 0)
        def _():
            out[:, :HALF] = mine[k]
            out[:, HALF:] = got[k]

        @pl.when(place[0] == 1)
        def _():
            out[:, :HALF] = got[k]
            out[:, HALF:] = mine[k]


def join(place, mine, got):
    n = mine.shape[0]
    return pl.pallas_call(
        join_kernel,
        in_specs=[IN_SMEM, IN_VMEM, IN_VMEM],
        out_specs=[IN_VMEM] * n,
        out_shape=[jax.ShapeDtypeStruct((FEAT // 2, FF), BF)] * n,
        compiler_params=params(),
        cost_estimate=cost(mine.size, 8 * mine.size),
    )(place, mine, got)


def cut_kernel(kept, got, far_a, far_b, above, below, own):
    n = FEAT // 2
    far = add(kept.at[0], got.at[0])
    far_a[...] = far[:n]
    far_b[...] = far[n:]
    for k, out in enumerate((above, below)):
        total = add(kept.at[1 + k], got.at[1 + k])
        out[0] = total[:n]
        out[1] = total[n:]
    own[0] = add(kept.at[3], got.at[3])


def cut(kept, got, *earlier):
    n = FEAT // 2
    shapes = [(n, HALF)] * 2 + [(2, n, HALF)] * 2 + [(1, FEAT, HALF)]
    return call(cut_kernel, [], [kept, got], shapes, kept.size, earlier)


def local(tokens, cotangent, expert_ids, combine, w_gate, w_up, w_down):
    dp = lax.axis_index("dp")
    place = jnp.stack([dp % 2, (dp // 2) % 2, dp // 4]).astype(jnp.int32)
    ids, weight = expert_ids.T, combine.reshape(1, -1)

    sel = select(ids, weight, tokens, cotangent)
    zhi, up0, down0 = to_zhi(sel), to_y(sel, -1), to_y(sel, 1)
    far0, down1 = to_y(down0, 1), to_zhi(down0)
    up1 = to_y(after(zhi, up0), -1)
    w_gate, w_up, w_down = stage([w_gate, w_up, w_down], up0, zhi)
    x_far1, d_far1 = split(up1, down1)
    x_far1, d_far1 = to_y(x_far1, -1), to_y(d_far1, 1)
    x_rows = gather_rows([far0, x_far1, up0, up1, down0, down1, sel, zhi])
    x_other = to_core(x_rows)
    hidden, hidden_sent, act, slope = gate_up(place, x_rows, w_gate, w_up)
    hidden_got = to_core(hidden_sent)
    d_chunks = [far0, d_far1, up0, up1, down0, down1, sel, zhi]
    d_rows, d_gate, d_up, d_sent = back_hidden(place, d_chunks, w_down, act, slope)
    d_got = to_core(d_sent)
    d_other = to_core(d_rows)
    out = out_terms(hidden, w_down, d_gate)

    far_a, far_b = gate_up_grads(place, [(2, None)], x_rows, x_other, d_gate, d_up, d_got, out)
    far_got_a, far_got_b = to_x(far_a, 1), to_x(far_b, -1)
    down_kept, down_sent = down_grads(place, d_rows, d_other, hidden, hidden_got, far_a)
    down_got = to_zlo(down_sent)
    row_far_a, row_far_b, row_above, row_below, row_own = row_terms(
        d_gate, d_up, w_gate, w_up, out, down_kept
    )
    row_got_a, row_got_b = to_y(row_far_a, 1), to_y(row_far_b, -1)
    above1, below1 = gate_up_grads(
        place, [(1, 1), (3, 1)], x_rows, x_other, d_gate, d_up, d_got, row_own
    )
    above0, below0, own0, own1 = gate_up_grads(
        place, [(1, 0), (3, 0), (0, None)], x_rows, x_other, d_gate, d_up, d_got, above1
    )
    below1, above0 = add_pairs(below1, far_got_b, above0, far_got_a)
    row_above, row_below = add_into(row_above, row_got_a, row_below, row_got_b, above0)
    above1, below1 = to_x(after(above1, above0), 1), to_x(below1, -1)
    row_above, row_below = to_y(row_above, 1), to_y(row_below, -1)
    sum1 = add_all(own1, above1, below1)
    far_a, far_b, above, below, down_own = cut(down_kept, down_got, sum1)
    above0, below0, *_ = lax.optimization_barrier((above0, below0, above1, below1, down_got))
    above0, below0 = to_x(above0, 1), to_x(below0, -1)
    sum1 = to_zlo(sum1)
    far_a, far_b = to_x(far_a, 1), to_x(far_b, -1)
    row_kept, row_sent = add_three(row_own, row_above, row_below)
    row_got = to_zhi(row_sent)
    expert_output, token_grad = place_rows(ids, weight, row_kept, row_got)
    mine, theirs = halves(place, own0, above0, below0, sum1)
    gate_grad, up_grad = join(place, mine, to_core(theirs))
    above, below = add_into(above, far_a, below, far_b)
    whole = lambda v: v.reshape(1, FEAT, HALF)
    above, below = whole(to_x(above, 1)), whole(to_x(below, -1))
    mine, theirs = halves(place, down_own, above, below)
    (down_grad,) = join(place, mine, to_core(theirs))
    return (expert_output, token_grad, gate_grad, up_grad, down_grad.T)


def solution(mesh):
    placed = (
        P(("dp", "tensor"), None),
        P(("dp", "tensor"), None),
        P(("dp", "tensor"), None),
        P(("dp", "tensor")),
        P(None, "tensor"),
        P(None, "tensor"),
        P("tensor", None),
    )
    return jax.shard_map(
        local,
        mesh=mesh,
        in_specs=placed,
        out_specs=(
            P(("dp", "tensor"), None),
            P(("dp", "tensor"), None),
            P("dp", "tensor"),
            P("dp", "tensor"),
            P("tensor", "dp"),
        ),
        check_vma=False,
    )
```

```python
import functools
import itertools
import math

import jax
import jax.numpy as jnp
from jax import lax
from jax.experimental import pallas as pl
from jax.experimental.pallas import tpu as pltpu
from jax.sharding import PartitionSpec as P

SLOTS = 48
ROWS = 384
DW = 3072
FF = 1024
HALF = 512
FEAT = 384
BF = jnp.bfloat16
F32 = jnp.float32
VMEM = 10 * 1024 * 1024
COST = 1000

IN_VMEM = pl.BlockSpec(memory_space=pltpu.VMEM)
IN_SMEM = pl.BlockSpec(memory_space=pltpu.SMEM)
IN_HBM = pl.BlockSpec(memory_space=pltpu.HBM)

DIM = (4, 2, 2, 2, 4)


def linear(place):
    r = 0
    for q, n in zip(place, DIM):
        r = r * n + q % n
    return r


def shift(value, axis, by):
    pairs = []
    for place in itertools.product(*map(range, DIM)):
        to = list(place)
        to[axis] += by
        pairs.append((linear(place), linear(to)))
    return lax.ppermute(value, ("dp", "tensor"), pairs)


to_x = lambda v, by: shift(v, 0, by)
to_zlo = lambda v: shift(v, 1, 1)
to_core = lambda v: shift(v, 2, 1)
to_zhi = lambda v: shift(v, 3, 1)
to_y = lambda v, by: shift(v, 4, by)


def dot(a, b):
    return jnp.dot(a, b, preferred_element_type=F32)


def dot_t(a, b):
    return lax.dot_general(a, b, (((1,), (1,)), ((), ())), preferred_element_type=F32)


def t_dot(a, b):
    return lax.dot_general(a, b, (((0,), (0,)), ((), ())), preferred_element_type=F32)


def cost(flops, nbytes):
    return pl.CostEstimate(flops=int(flops / COST), bytes_accessed=int(nbytes / COST), transcendentals=0)


def params():
    return pltpu.CompilerParams(vmem_limit_bytes=VMEM)


def after(value, *others):
    return lax.optimization_barrier((value, *others))[0]


def picks_of(ids, weight):
    n = ids.shape[1]
    chosen = (ids[0:1] == 0) | (ids[1:2] == 0)
    ones = jnp.where(chosen, 1.0, 0.0).astype(BF)
    before = lax.broadcasted_iota(jnp.int32, (n, n), 0) <= lax.broadcasted_iota(jnp.int32, (n, n), 1)
    place = dot(jnp.broadcast_to(ones, (8, n)), jnp.where(before, 1.0, 0.0).astype(BF))[0:1]
    place = place.astype(jnp.int32) - 1
    slot = lax.broadcasted_iota(jnp.int32, (SLOTS, n), 0)
    picks = jnp.where((place == slot) & chosen, 1.0, 0.0)
    return picks.astype(BF), jnp.sum(picks * weight, axis=1, keepdims=True)


def select_kernel(ids, weight, x, d, out, ids_here, weight_here, x_here, d_here, sems):
    copies = [
        pltpu.make_async_copy(far, near, sems.at[k])
        for k, (far, near) in enumerate(
            ((ids, ids_here), (weight, weight_here), (x, x_here), (d, d_here))
        )
    ]
    for copy in copies:
        copy.start()
    copies[0].wait()
    copies[1].wait()
    picks, slot_weight = picks_of(ids_here[...], weight_here[...])
    copies[2].wait()
    out[0] = dot(picks, x_here[...]).astype(BF)
    copies[3].wait()
    out[1] = (dot(picks, d_here[...]) * slot_weight).astype(BF)


def in_hbm(array):
    return pltpu.with_memory_space_constraint(array, pltpu.HBM)


def select(*arrays):
    return pl.pallas_call(
        select_kernel,
        in_specs=[IN_HBM] * 4,
        out_specs=IN_VMEM,
        out_shape=pltpu.VMEM((2, SLOTS, DW), BF),
        scratch_shapes=[pltpu.VMEM(a.shape, a.dtype) for a in arrays]
        + [pltpu.SemaphoreType.DMA((4,))],
        compiler_params=params(),
        cost_estimate=cost(4 * SLOTS * 128 * DW, 2.2e6),
    )(*map(in_hbm, arrays))


def place_kernel(ids, weight, kept, got, output, token_grad):
    picks, slot_weight = picks_of(ids[...], weight[...])
    out = kept[0].astype(F32) + got[0].astype(F32)
    output[...] = t_dot(picks, (out * slot_weight).astype(BF)).astype(BF)
    back = kept[1].astype(F32) + got[1].astype(F32)
    token_grad[...] = t_dot(picks, back.astype(BF)).astype(BF)


def place_rows(ids, weight, kept, got):
    return pl.pallas_call(
        place_kernel,
        in_specs=[IN_VMEM] * 4,
        out_specs=[IN_VMEM] * 2,
        out_shape=[jax.ShapeDtypeStruct((128, DW), BF)] * 2,
        compiler_params=params(),
        cost_estimate=cost(4 * SLOTS * 128 * DW, 2.8e6),
    )(ids, weight, kept, got)


IN_ANY = pl.BlockSpec(memory_space=pl.ANY)


def without(first, count, kernel):
    def run(*refs):
        kernel(*refs[:first], *refs[first + count :])

    return run


def call(kernel, scalars, arrays, shapes, flops, earlier=(), hbm=(), scratch=(), aliases=None):
    shapes = [s if isinstance(s[0], tuple) else (s, BF) for s in shapes]
    size = sum(a.size for a in arrays) + sum(math.prod(s) for s, _ in shapes)
    inputs = len(scalars) + len(arrays) + len(hbm)
    return pl.pallas_call(
        without(inputs, len(earlier), kernel),
        in_specs=[IN_SMEM] * len(scalars)
        + [IN_VMEM] * len(arrays)
        + [IN_HBM] * len(hbm)
        + [IN_ANY] * len(earlier),
        out_specs=[IN_VMEM] * len(shapes),
        out_shape=[pltpu.VMEM(s, t) for s, t in shapes],
        scratch_shapes=list(scratch),
        input_output_aliases=aliases or {},
        compiler_params=params(),
        cost_estimate=cost(flops, size),
    )(*scalars, *arrays, *map(in_hbm, hbm), *earlier)


def stage_kernel(n, *refs):
    *refs, token, sems = refs
    copies = [pltpu.make_async_copy(refs[i], refs[n + i], sems.at[i]) for i in range(n)]
    for copy in copies:
        copy.start()
    token[...] = jnp.zeros_like(token)
    for copy in copies:
        copy.wait()


def stage(arrays, *earlier):
    return call(
        functools.partial(stage_kernel, len(arrays)),
        [],
        [],
        [a.shape for a in arrays] + [((8, 128), F32)],
        1,
        earlier,
        hbm=arrays,
        scratch=[pltpu.SemaphoreType.DMA((len(arrays),))],
    )


def place_of():
    dp = lax.axis_index("dp")
    return dp % 2, (dp // 2) % 2, dp // 4


def half(h):
    return pl.ds(pl.multiple_of(h * HALF, HALF), HALF)


def pack_kernel(*refs):
    *chunks, out = refs
    for k, chunk in enumerate(chunks):
        out[:, k * SLOTS : (k + 1) * SLOTS] = chunk[...]


def pack(*chunks, earlier=()):
    return call(pack_kernel, [], chunks, [(2, SLOTS * len(chunks), DW)], 1, earlier)[0]


def pair_kernel(x, d, out):
    out[0] = x[...]
    out[1] = d[...]


def pair(x, d):
    return call(pair_kernel, [], [x, d], [(2, SLOTS, DW)], 1)[0]


def split_kernel(a, b, x, d):
    x[...] = a[0]
    d[...] = b[1]


def split(a, b, *earlier):
    return call(split_kernel, [], [a, b], [(SLOTS, DW)] * 2, 1, earlier)


FIRST = ROWS - SLOTS


def gate_rows(r, rows, w_gate, w_up, hidden, act, slope):
    for h in range(2):
        at = slice(h * HALF, (h + 1) * HALF)
        gate = dot(rows[...], w_gate[:, at])
        up = dot(rows[...], w_up[:, at])
        s = jax.nn.sigmoid(gate)
        silu = gate * s
        act[r, at] = silu
        slope[r, at] = up * s * (1.0 + gate * (1.0 - s))
        hidden[r, at] = (silu * up).astype(BF)


GATE_SHAPES = [(ROWS, FF), ((ROWS, FF), F32), ((ROWS, FF), F32)]


def gate_first_kernel(a, b, w_gate, w_up, hidden, act, slope, rows):
    n = a.shape[1]
    rows[:n] = a[0]
    rows[n:] = b[0]
    gate_rows(slice(0, FIRST), rows, w_gate, w_up, hidden, act, slope)


def gate_first(a, b, w_gate, w_up, *earlier):
    return call(
        gate_first_kernel,
        [],
        [a, b, w_gate, w_up],
        GATE_SHAPES,
        4 * FIRST * DW * FF,
        earlier,
        scratch=[pltpu.VMEM((FIRST, DW), BF)],
    )


def gate_last_kernel(chunk, w_gate, w_up, *refs):
    hidden, act, slope = refs[3:]
    gate_rows(slice(FIRST, ROWS), chunk, w_gate, w_up, hidden, act, slope)


def gate_last(chunk, w_gate, w_up, first, *earlier):
    return call(
        gate_last_kernel,
        [],
        [chunk, w_gate, w_up, *first],
        GATE_SHAPES,
        4 * SLOTS * DW * FF,
        earlier,
        aliases={3 + k: k for k in range(3)},
    )


def back_half(mine, rows, w_down, act, slope, out):
    at = half(mine)
    d_hidden = dot_t(rows[...], w_down[at, :])
    out[0] = (d_hidden * slope[:, at]).astype(BF)
    out[1] = (d_hidden * act[:, at]).astype(BF)


def back_other_kernel(a, b, last, w_down, hidden, act, slope, rows, out):
    n = a.shape[1]
    rows[:n] = a[1]
    rows[n:FIRST] = b[1]
    rows[FIRST:] = last[...]
    other = 1 - place_of()[0]
    out[2] = hidden[:, half(other)]
    back_half(other, rows, w_down, act, slope, out)


def back_other(a, b, last, w_down, hidden, act, slope):
    arrays = [a, b, last, w_down, hidden, act, slope]
    shapes = [(ROWS, DW), (3, ROWS, HALF)]
    return call(back_other_kernel, [], arrays, shapes, ROWS * DW * FF)


def back_own_kernel(rows, w_down, act, slope, out):
    back_half(place_of()[0], rows, w_down, act, slope, out)


def back_own(rows, w_down, act, slope):
    shapes = [(2, ROWS, HALF)]
    return call(back_own_kernel, [], [rows, w_down, act, slope], shapes, ROWS * DW * FF)[0]


def out_kernel(hidden, w_down, out):
    for j in range(0, DW, 768):
        at = slice(j, j + 768)
        out[:, at] = dot(hidden[...], w_down[:, at]).astype(BF)


def out_terms(hidden, w_down, *earlier):
    return call(out_kernel, [], [hidden, w_down], [(ROWS, DW)], 2 * ROWS * DW * FF, earlier)[0]


def token_kernel(mine, other, w_gate, w_up, out, far_a, far_b, above, below, own):
    targets = [above.at[0], below.at[0], own.at[0], own.at[1], far_a, above.at[1], below.at[1], far_b]
    core = place_of()[0]
    for j in range(0, DW, 768):
        at = slice(j, j + 768)
        back = sum(
            dot_t(d[m], w[at, half(h)])
            for d, h in ((mine, core), (other, 1 - core))
            for m, w in enumerate((w_gate, w_up))
        )
        for k, target in enumerate(targets):
            rows = slice(k * SLOTS, (k + 1) * SLOTS)
            target[0, :, at] = out[rows, at]
            target[1, :, at] = back[rows].astype(BF)


def row_terms(mine, other, w_gate, w_up, out, *earlier):
    shapes = [(2, SLOTS, DW)] * 2 + [(2, 2, SLOTS, DW)] * 3
    return call(
        token_kernel, [], [mine, other, w_gate, w_up, out], shapes, 4 * ROWS * DW * FF, earlier
    )


def both(*rows):
    return jnp.concatenate(rows, axis=0)


def features(place, dx):
    at = ((place[2] + dx) % 4) * (2 * FEAT)
    return pl.ds(pl.multiple_of(at, 2 * FEAT), 2 * FEAT)


def store_pair(place, first, second, low, high):
    @pl.when(place[1] == 0)
    def _():
        first[...] = low
        second[...] = high

    @pl.when(place[1] == 1)
    def _():
        first[...] = high
        second[...] = low


def rows_at(which, parts, at):
    return both(*(p[which, :, at] for p in parts))


def grads_kernel(pairs, *refs):
    x_parts, (mine, got, *outs) = refs[:6], refs[6:]
    place = place_of()
    terms = [both(mine[m], got[m]) for m in range(2)]
    for dx, dz in pairs:
        if dz is None:
            at = features(place, dx)
        else:
            at = ((place[2] + dx) % 4) * (2 * FEAT) + ((place[1] + dz) % 2) * FEAT
            at = pl.ds(pl.multiple_of(at, FEAT), FEAT)
        x = rows_at(0, x_parts, at)
        here = [outs.pop(0) for _ in range(2 if dz is None else 1)]
        for m in range(2):
            result = t_dot(x, terms[m]).astype(BF)
            if dz is None:
                store_pair(place, here[0].at[m], here[1].at[m], result[:FEAT], result[FEAT:])
            else:
                here[0][m] = result


def gate_up_grads(pairs, x_parts, mine, got, *earlier):
    n = sum(2 if dz is None else 1 for _, dz in pairs)
    return call(
        functools.partial(grads_kernel, pairs),
        [],
        [*x_parts, mine, got],
        [(2, FEAT, HALF)] * n,
        n * ROWS * DW * FF / 2,
        earlier,
    )


def down_kernel(*refs):
    d_parts, (hidden, got, kept, sent) = refs[:6], refs[6:]
    place = place_of()
    h = both(hidden[:, half(place[0])], got[2])
    for k, dx in enumerate((2, 1, 3, 0)):
        at = features(place, dx)
        result = t_dot(rows_at(1, d_parts, at), h).astype(BF)
        store_pair(place, kept.at[k], sent.at[k], result[:FEAT], result[FEAT:])


def down_grads(parts, hidden, got, *earlier):
    shapes = [(4, FEAT, HALF)] * 2
    return call(down_kernel, [], [*parts, hidden, got], shapes, 2 * ROWS * DW * FF, earlier)


def add(*terms):
    return sum(t[...].astype(F32) for t in terms).astype(BF)


def add_pairs_kernel(n, *refs):
    for k in range(n):
        refs[2 * n + k][...] = add(refs[2 * k], refs[2 * k + 1])


def add_pairs(*terms):
    n = len(terms) // 2
    shapes = [t.shape for t in terms[::2]]
    flops = sum(math.prod(s) for s in shapes)
    return call(functools.partial(add_pairs_kernel, n), [], terms, shapes, flops)


def add_all_kernel(*refs):
    refs[-1][...] = add(*refs[:-1])


def add_all(*terms):
    return call(add_all_kernel, [], terms, [terms[0].shape], 2 * terms[0].size)[0]


def add_into_kernel(above, got_a, below, got_b, new_above, new_below):
    new_above[0] = add(above.at[0], got_a)
    new_above[1] = above[1]
    new_below[0] = below[0]
    new_below[1] = add(below.at[1], got_b)


def add_into(above, got_a, below, got_b, *earlier):
    return call(
        add_into_kernel, [], [above, got_a, below, got_b], [above.shape] * 2, above.size, earlier
    )


def add_three_kernel(own, above, below, kept, sent):
    kept[...] = add(own.at[0], above.at[0], below.at[0])
    sent[...] = add(own.at[1], above.at[1], below.at[1])


def add_three(own, above, below):
    return call(add_three_kernel, [], [own, above, below], [own.shape[1:]] * 2, 2 * own.size)


def halves_kernel(*refs):
    *terms, mine, theirs = refs
    place = place_of()
    total = add(*terms)
    low, high = total[:, : FEAT // 2], total[:, FEAT // 2 :]

    @pl.when(place[0] == 0)
    def _():
        mine[...] = low
        theirs[...] = high

    @pl.when(place[0] == 1)
    def _():
        mine[...] = high
        theirs[...] = low


def halves(*terms):
    n = terms[0].shape[0]
    return call(halves_kernel, [], terms, [(n, FEAT // 2, HALF)] * 2, 2 * terms[0].size)


def join_kernel(mine, got, *outs):
    place = place_of()
    for k, out in enumerate(outs):

        @pl.when(place[0] == 0)
        def _():
            out[:, :HALF] = mine[k]
            out[:, HALF:] = got[k]

        @pl.when(place[0] == 1)
        def _():
            out[:, :HALF] = got[k]
            out[:, HALF:] = mine[k]


def join(mine, got):
    n = mine.shape[0]
    return pl.pallas_call(
        join_kernel,
        in_specs=[IN_VMEM, IN_VMEM],
        out_specs=[IN_VMEM] * n,
        out_shape=[jax.ShapeDtypeStruct((FEAT // 2, FF), BF)] * n,
        compiler_params=params(),
        cost_estimate=cost(mine.size, 8 * mine.size),
    )(mine, got)


def cut_kernel(kept, got, far_a, far_b, above, below, own):
    n = FEAT // 2
    far = add(kept.at[0], got.at[0])
    far_a[...] = far[:n]
    far_b[...] = far[n:]
    for k, out in enumerate((above, below)):
        total = add(kept.at[1 + k], got.at[1 + k])
        out[0] = total[:n]
        out[1] = total[n:]
    own[0] = add(kept.at[3], got.at[3])


def cut(kept, got, *earlier):
    n = FEAT // 2
    shapes = [(n, HALF)] * 2 + [(2, n, HALF)] * 2 + [(1, FEAT, HALF)]
    return call(cut_kernel, [], [kept, got], shapes, kept.size, earlier)


def local(tokens, cotangent, expert_ids, combine, w_gate, w_up, w_down):
    ids, weight = expert_ids.T, combine.reshape(1, -1)

    sel = select(ids, weight, tokens, cotangent)
    zhi, up0, down0 = to_zhi(sel), to_y(sel, -1), to_y(sel, 1)
    far0, down1 = to_y(down0, 1), to_zhi(down0)
    up1 = to_y(after(zhi, up0), -1)
    w_gate, w_up, w_down, there = stage([w_gate, w_up, w_down], up0, zhi)
    four = pack(up0, down0, sel, zhi, earlier=[there])
    x_far1, d_far1 = split(up1, down1, there)
    three = pack(far0, up1, down1)
    first = gate_first(four, three, w_gate, w_up, x_far1)
    x_far1, d_far1 = to_y(x_far1, -1), to_y(d_far1, 1)
    four_other, three_other = to_core(four), to_core(three)
    far1 = pair(x_far1, d_far1)
    parts = [four, three, far1, four_other, three_other, to_core(far1)]
    hidden, act, slope = gate_last(x_far1, w_gate, w_up, first, four_other, three_other)
    d_rows, d_sent = back_other(four, three, d_far1, w_down, hidden, act, slope)
    d_got = to_core(d_sent)
    d_mine = back_own(d_rows, w_down, act, slope)

    down_kept, down_sent = down_grads(parts, hidden, d_got, d_mine)
    down_got = to_zlo(down_sent)
    far_a, far_b = gate_up_grads([(2, None)], parts, d_mine, d_got, down_kept)
    far_got_a, far_got_b = to_x(far_a, 1), to_x(far_b, -1)
    out = out_terms(hidden, w_down, far_a)
    row_far_a, row_far_b, row_above, row_below, row_own = row_terms(
        d_mine, d_sent, w_gate, w_up, out
    )
    row_got_a, row_got_b = to_y(row_far_a, 1), to_y(row_far_b, -1)
    above1, below1 = gate_up_grads([(1, 1), (3, 1)], parts, d_mine, d_got, row_own)
    (below1,) = add_pairs(below1, far_got_b)
    above1 = after(above1, below1)
    above0, below0, own0, own1 = gate_up_grads(
        [(1, 0), (3, 0), (0, None)], parts, d_mine, d_got, below1
    )
    above1, below1 = to_x(above1, 1), to_x(below1, -1)
    (above0,) = add_pairs(above0, far_got_a)
    row_above, row_below = add_into(row_above, row_got_a, row_below, row_got_b, above0)
    row_above, row_below = to_y(row_above, 1), to_y(row_below, -1)
    sum1 = add_all(own1, above1, below1)
    far_a, far_b, above, below, down_own = cut(down_kept, down_got, sum1)
    above0, below0, *_ = lax.optimization_barrier((above0, below0, above1, below1, down_got))
    above0, below0 = to_x(above0, 1), to_x(below0, -1)
    sum1 = to_zlo(sum1)
    far_a, far_b = to_x(far_a, 1), to_x(far_b, -1)
    row_kept, row_sent = add_three(row_own, row_above, row_below)
    row_got = to_zhi(row_sent)
    expert_output, token_grad = place_rows(ids, weight, row_kept, row_got)
    mine, theirs = halves(own0, above0, below0, sum1)
    gate_grad, up_grad = join(mine, to_core(theirs))
    above, below = add_into(above, far_a, below, far_b)
    whole = lambda v: v.reshape(1, FEAT, HALF)
    above, below = whole(to_x(above, 1)), whole(to_x(below, -1))
    mine, theirs = halves(down_own, above, below)
    (down_grad,) = join(mine, to_core(theirs))
    return (expert_output, token_grad, gate_grad, up_grad, down_grad.T)


def solution(mesh):
    placed = (
        P(("dp", "tensor"), None),
        P(("dp", "tensor"), None),
        P(("dp", "tensor"), None),
        P(("dp", "tensor")),
        P(None, "tensor"),
        P(None, "tensor"),
        P("tensor", None),
    )
    return jax.shard_map(
        local,
        mesh=mesh,
        in_specs=placed,
        out_specs=(
            P(("dp", "tensor"), None),
            P(("dp", "tensor"), None),
            P("dp", "tensor"),
            P("dp", "tensor"),
            P("tensor", "dp"),
        ),
        check_vma=False,
    )
```

```python
import functools
import itertools
import math

import jax
import jax.numpy as jnp
from jax import lax
from jax.experimental import pallas as pl
from jax.experimental.pallas import tpu as pltpu
from jax.sharding import PartitionSpec as P

SLOTS = 48
ROWS = 384
DW = 3072
FF = 1024
HALF = 512
FEAT = 384
BF = jnp.bfloat16
F32 = jnp.float32
VMEM = 10 * 1024 * 1024
COST = 1000

IN_VMEM = pl.BlockSpec(memory_space=pltpu.VMEM)
IN_SMEM = pl.BlockSpec(memory_space=pltpu.SMEM)
IN_HBM = pl.BlockSpec(memory_space=pltpu.HBM)

DIM = (4, 2, 2, 2, 4)


def linear(place):
    r = 0
    for q, n in zip(place, DIM):
        r = r * n + q % n
    return r


def shift(value, axis, by):
    pairs = []
    for place in itertools.product(*map(range, DIM)):
        to = list(place)
        to[axis] += by
        pairs.append((linear(place), linear(to)))
    return lax.ppermute(value, ("dp", "tensor"), pairs)


to_x = lambda v, by: shift(v, 0, by)
to_zlo = lambda v: shift(v, 1, 1)
to_core = lambda v: shift(v, 2, 1)
to_zhi = lambda v: shift(v, 3, 1)
to_y = lambda v, by: shift(v, 4, by)


def dot(a, b):
    return jnp.dot(a, b, preferred_element_type=F32)


def dot_t(a, b):
    return lax.dot_general(a, b, (((1,), (1,)), ((), ())), preferred_element_type=F32)


def t_dot(a, b):
    return lax.dot_general(a, b, (((0,), (0,)), ((), ())), preferred_element_type=F32)


def cost(flops, nbytes):
    return pl.CostEstimate(flops=int(flops / COST), bytes_accessed=int(nbytes / COST), transcendentals=0)


def params():
    return pltpu.CompilerParams(vmem_limit_bytes=VMEM)


def after(value, *others):
    return lax.optimization_barrier((value, *others))[0]


def picks_of(ids, weight):
    n = ids.shape[1]
    chosen = (ids[0:1] == 0) | (ids[1:2] == 0)
    ones = jnp.where(chosen, 1.0, 0.0).astype(BF)
    before = lax.broadcasted_iota(jnp.int32, (n, n), 0) <= lax.broadcasted_iota(jnp.int32, (n, n), 1)
    place = dot(jnp.broadcast_to(ones, (8, n)), jnp.where(before, 1.0, 0.0).astype(BF))[0:1]
    place = place.astype(jnp.int32) - 1
    slot = lax.broadcasted_iota(jnp.int32, (SLOTS, n), 0)
    picks = jnp.where((place == slot) & chosen, 1.0, 0.0)
    return picks.astype(BF), jnp.sum(picks * weight, axis=1, keepdims=True)


def select_kernel(ids, weight, x, d, out, ids_here, weight_here, x_here, d_here, sems):
    copies = [
        pltpu.make_async_copy(far, near, sems.at[k])
        for k, (far, near) in enumerate(
            ((ids, ids_here), (weight, weight_here), (x, x_here), (d, d_here))
        )
    ]
    for copy in copies:
        copy.start()
    copies[0].wait()
    copies[1].wait()
    picks, slot_weight = picks_of(ids_here[...], weight_here[...])
    copies[2].wait()
    out[0] = dot(picks, x_here[...]).astype(BF)
    copies[3].wait()
    out[1] = (dot(picks, d_here[...]) * slot_weight).astype(BF)


def in_hbm(array):
    return pltpu.with_memory_space_constraint(array, pltpu.HBM)


def select(*arrays):
    return pl.pallas_call(
        select_kernel,
        in_specs=[IN_HBM] * 4,
        out_specs=IN_VMEM,
        out_shape=pltpu.VMEM((2, SLOTS, DW), BF),
        scratch_shapes=[pltpu.VMEM(a.shape, a.dtype) for a in arrays]
        + [pltpu.SemaphoreType.DMA((4,))],
        compiler_params=params(),
        cost_estimate=cost(4 * SLOTS * 128 * DW, 2.2e6),
    )(*map(in_hbm, arrays))


def place_kernel(ids, weight, kept, got, output, token_grad):
    picks, slot_weight = picks_of(ids[...], weight[...])
    out = kept[0].astype(F32) + got[0].astype(F32)
    output[...] = t_dot(picks, (out * slot_weight).astype(BF)).astype(BF)
    back = kept[1].astype(F32) + got[1].astype(F32)
    token_grad[...] = t_dot(picks, back.astype(BF)).astype(BF)


def place_rows(ids, weight, kept, got):
    return pl.pallas_call(
        place_kernel,
        in_specs=[IN_VMEM] * 4,
        out_specs=[IN_VMEM] * 2,
        out_shape=[jax.ShapeDtypeStruct((128, DW), BF)] * 2,
        compiler_params=params(),
        cost_estimate=cost(4 * SLOTS * 128 * DW, 2.8e6),
    )(ids, weight, kept, got)


IN_ANY = pl.BlockSpec(memory_space=pl.ANY)


def without(first, count, kernel):
    def run(*refs):
        kernel(*refs[:first], *refs[first + count :])

    return run


def call(kernel, scalars, arrays, shapes, flops, earlier=(), hbm=(), scratch=(), aliases=None):
    shapes = [s if isinstance(s[0], tuple) else (s, BF) for s in shapes]
    size = sum(a.size for a in arrays) + sum(math.prod(s) for s, _ in shapes)
    inputs = len(scalars) + len(arrays) + len(hbm)
    return pl.pallas_call(
        without(inputs, len(earlier), kernel),
        in_specs=[IN_SMEM] * len(scalars)
        + [IN_VMEM] * len(arrays)
        + [IN_HBM] * len(hbm)
        + [IN_ANY] * len(earlier),
        out_specs=[IN_VMEM] * len(shapes),
        out_shape=[pltpu.VMEM(s, t) for s, t in shapes],
        scratch_shapes=list(scratch),
        input_output_aliases=aliases or {},
        compiler_params=params(),
        cost_estimate=cost(flops, size),
    )(*scalars, *arrays, *map(in_hbm, hbm), *earlier)


def stage_kernel(n, *refs):
    *refs, token, sems = refs
    copies = [pltpu.make_async_copy(refs[i], refs[n + i], sems.at[i]) for i in range(n)]
    for copy in copies:
        copy.start()
    token[...] = jnp.zeros_like(token)
    for copy in copies:
        copy.wait()


def stage(arrays, *earlier):
    return call(
        functools.partial(stage_kernel, len(arrays)),
        [],
        [],
        [a.shape for a in arrays] + [((8, 128), F32)],
        1,
        earlier,
        hbm=arrays,
        scratch=[pltpu.SemaphoreType.DMA((len(arrays),))],
    )


def place_of():
    dp = lax.axis_index("dp")
    return dp % 2, (dp // 2) % 2, dp // 4


def half(h):
    return pl.ds(pl.multiple_of(h * HALF, HALF), HALF)


def pack_kernel(*refs):
    *chunks, out = refs
    for k, chunk in enumerate(chunks):
        out[:, k * SLOTS : (k + 1) * SLOTS] = chunk[...]


def pack(*chunks, earlier=()):
    return call(pack_kernel, [], chunks, [(2, SLOTS * len(chunks), DW)], 1, earlier)[0]


def pair_kernel(x, d, out):
    out[0] = x[...]
    out[1] = d[...]


def pair(x, d):
    return call(pair_kernel, [], [x, d], [(2, SLOTS, DW)], 1)[0]


def split_kernel(which, chunk, out):
    out[...] = chunk[which]


def split(which, chunk, *earlier):
    kernel = functools.partial(split_kernel, which)
    return call(kernel, [], [chunk], [(SLOTS, DW)], 1, earlier)[0]


FIRST = ROWS - SLOTS


def gate_rows(r, rows, w_gate, w_up, hidden, act, slope):
    for h in range(2):
        at = slice(h * HALF, (h + 1) * HALF)
        gate = dot(rows[...], w_gate[:, at])
        up = dot(rows[...], w_up[:, at])
        s = jax.nn.sigmoid(gate)
        silu = gate * s
        act[r, at] = silu
        slope[r, at] = up * s * (1.0 + gate * (1.0 - s))
        hidden[r, at] = (silu * up).astype(BF)


GATE_SHAPES = [(ROWS, FF), ((ROWS, FF), F32), ((ROWS, FF), F32)]


def gate_first_kernel(a, b, w_gate, w_up, hidden, act, slope, rows):
    n = a.shape[1]
    rows[:n] = a[0]
    rows[n:] = b[0]
    gate_rows(slice(0, FIRST), rows, w_gate, w_up, hidden, act, slope)


def gate_first(a, b, w_gate, w_up, *earlier):
    return call(
        gate_first_kernel,
        [],
        [a, b, w_gate, w_up],
        GATE_SHAPES,
        4 * FIRST * DW * FF,
        earlier,
        scratch=[pltpu.VMEM((FIRST, DW), BF)],
    )


def gate_last_kernel(chunk, w_gate, w_up, *refs):
    hidden, act, slope = refs[3:]
    gate_rows(slice(FIRST, ROWS), chunk, w_gate, w_up, hidden, act, slope)


def gate_last(chunk, w_gate, w_up, first, *earlier):
    return call(
        gate_last_kernel,
        [],
        [chunk, w_gate, w_up, *first],
        GATE_SHAPES,
        4 * SLOTS * DW * FF,
        earlier,
        aliases={3 + k: k for k in range(3)},
    )


def back_half(mine, rows, w_down, act, slope, out):
    at = half(mine)
    d_hidden = dot_t(rows[...], w_down[at, :])
    out[0] = (d_hidden * slope[:, at]).astype(BF)
    out[1] = (d_hidden * act[:, at]).astype(BF)


def back_other_kernel(a, b, last, w_down, hidden, act, slope, rows, out):
    n = a.shape[1]
    rows[:n] = a[1]
    rows[n:FIRST] = b[1]
    rows[FIRST:] = last[...]
    other = 1 - place_of()[0]
    out[2] = hidden[:, half(other)]
    back_half(other, rows, w_down, act, slope, out)


def back_other(a, b, last, w_down, hidden, act, slope):
    arrays = [a, b, last, w_down, hidden, act, slope]
    shapes = [(ROWS, DW), (3, ROWS, HALF)]
    return call(back_other_kernel, [], arrays, shapes, ROWS * DW * FF)


def back_own_kernel(rows, w_down, act, slope, out):
    back_half(place_of()[0], rows, w_down, act, slope, out)


def back_own(rows, w_down, act, slope):
    shapes = [(2, ROWS, HALF)]
    return call(back_own_kernel, [], [rows, w_down, act, slope], shapes, ROWS * DW * FF)[0]


def out_kernel(hidden, w_down, out):
    for j in range(0, DW, 768):
        at = slice(j, j + 768)
        out[:, at] = dot(hidden[...], w_down[:, at]).astype(BF)


def out_terms(hidden, w_down, *earlier):
    return call(out_kernel, [], [hidden, w_down], [(ROWS, DW)], 2 * ROWS * DW * FF, earlier)[0]


def token_kernel(mine, other, w_gate, w_up, out, far_a, far_b, above, below, own):
    targets = [above.at[0], below.at[0], own.at[0], own.at[1], far_a, above.at[1], below.at[1], far_b]
    core = place_of()[0]
    for j in range(0, DW, 768):
        at = slice(j, j + 768)
        back = sum(
            dot_t(d[m], w[at, half(h)])
            for d, h in ((mine, core), (other, 1 - core))
            for m, w in enumerate((w_gate, w_up))
        )
        for k, target in enumerate(targets):
            rows = slice(k * SLOTS, (k + 1) * SLOTS)
            target[0, :, at] = out[rows, at]
            target[1, :, at] = back[rows].astype(BF)


def row_terms(mine, other, w_gate, w_up, out, *earlier):
    shapes = [(2, SLOTS, DW)] * 2 + [(2, 2, SLOTS, DW)] * 3
    return call(
        token_kernel, [], [mine, other, w_gate, w_up, out], shapes, 4 * ROWS * DW * FF, earlier
    )


def both(*rows):
    return jnp.concatenate(rows, axis=0)


def features(place, dx):
    at = ((place[2] + dx) % 4) * (2 * FEAT)
    return pl.ds(pl.multiple_of(at, 2 * FEAT), 2 * FEAT)


def store_pair(place, first, second, low, high):
    @pl.when(place[1] == 0)
    def _():
        first[...] = low
        second[...] = high

    @pl.when(place[1] == 1)
    def _():
        first[...] = high
        second[...] = low


def rows_at(which, parts, at):
    return both(*(p[which, :, at] for p in parts))


def grads_kernel(pairs, *refs):
    x_parts, (mine, got, *outs) = refs[:6], refs[6:]
    place = place_of()
    terms = [both(mine[m], got[m]) for m in range(2)]
    for dx, dz in pairs:
        if dz is None:
            at = features(place, dx)
        else:
            at = ((place[2] + dx) % 4) * (2 * FEAT) + ((place[1] + dz) % 2) * FEAT
            at = pl.ds(pl.multiple_of(at, FEAT), FEAT)
        x = rows_at(0, x_parts, at)
        here = [outs.pop(0) for _ in range(2 if dz is None else 1)]
        for m in range(2):
            result = t_dot(x, terms[m]).astype(BF)
            if dz is None:
                store_pair(place, here[0].at[m], here[1].at[m], result[:FEAT], result[FEAT:])
            else:
                here[0][m] = result


def gate_up_grads(pairs, x_parts, mine, got, *earlier):
    n = sum(2 if dz is None else 1 for _, dz in pairs)
    return call(
        functools.partial(grads_kernel, pairs),
        [],
        [*x_parts, mine, got],
        [(2, FEAT, HALF)] * n,
        n * ROWS * DW * FF / 2,
        earlier,
    )


def down_kernel(*refs):
    d_parts, (hidden, got, kept, sent) = refs[:6], refs[6:]
    place = place_of()
    h = both(hidden[:, half(place[0])], got[2])
    for k, dx in enumerate((2, 1, 3, 0)):
        at = features(place, dx)
        result = t_dot(rows_at(1, d_parts, at), h).astype(BF)
        store_pair(place, kept.at[k], sent.at[k], result[:FEAT], result[FEAT:])


def down_grads(parts, hidden, got, *earlier):
    shapes = [(4, FEAT, HALF)] * 2
    return call(down_kernel, [], [*parts, hidden, got], shapes, 2 * ROWS * DW * FF, earlier)


def add(*terms):
    return sum(t[...].astype(F32) for t in terms).astype(BF)


def add_pairs_kernel(n, *refs):
    for k in range(n):
        refs[2 * n + k][...] = add(refs[2 * k], refs[2 * k + 1])


def add_pairs(*terms):
    n = len(terms) // 2
    shapes = [t.shape for t in terms[::2]]
    flops = sum(math.prod(s) for s in shapes)
    return call(functools.partial(add_pairs_kernel, n), [], terms, shapes, flops)


def add_all_kernel(*refs):
    refs[-1][...] = add(*refs[:-1])


def add_all(*terms):
    return call(add_all_kernel, [], terms, [terms[0].shape], 2 * terms[0].size)[0]


def add_into_kernel(above, got_a, below, got_b, new_above, new_below):
    new_above[0] = add(above.at[0], got_a)
    new_above[1] = above[1]
    new_below[0] = below[0]
    new_below[1] = add(below.at[1], got_b)


def add_into(above, got_a, below, got_b, *earlier):
    return call(
        add_into_kernel, [], [above, got_a, below, got_b], [above.shape] * 2, above.size, earlier
    )


def add_three_kernel(own, above, below, kept, sent):
    kept[...] = add(own.at[0], above.at[0], below.at[0])
    sent[...] = add(own.at[1], above.at[1], below.at[1])


def add_three(own, above, below):
    return call(add_three_kernel, [], [own, above, below], [own.shape[1:]] * 2, 2 * own.size)


def halves_kernel(*refs):
    *terms, mine, theirs = refs
    place = place_of()
    total = add(*terms)
    low, high = total[:, : FEAT // 2], total[:, FEAT // 2 :]

    @pl.when(place[0] == 0)
    def _():
        mine[...] = low
        theirs[...] = high

    @pl.when(place[0] == 1)
    def _():
        mine[...] = high
        theirs[...] = low


def halves(*terms):
    n = terms[0].shape[0]
    return call(halves_kernel, [], terms, [(n, FEAT // 2, HALF)] * 2, 2 * terms[0].size)


def join_kernel(mine, got, *outs):
    place = place_of()
    for k, out in enumerate(outs):

        @pl.when(place[0] == 0)
        def _():
            out[:, :HALF] = mine[k]
            out[:, HALF:] = got[k]

        @pl.when(place[0] == 1)
        def _():
            out[:, :HALF] = got[k]
            out[:, HALF:] = mine[k]


def join(mine, got):
    n = mine.shape[0]
    return pl.pallas_call(
        join_kernel,
        in_specs=[IN_VMEM, IN_VMEM],
        out_specs=[IN_VMEM] * n,
        out_shape=[jax.ShapeDtypeStruct((FEAT // 2, FF), BF)] * n,
        compiler_params=params(),
        cost_estimate=cost(mine.size, 8 * mine.size),
    )(mine, got)


def cut_kernel(kept, got, far_a, far_b, above, below, own):
    n = FEAT // 2
    far = add(kept.at[0], got.at[0])
    far_a[...] = far[:n]
    far_b[...] = far[n:]
    for k, out in enumerate((above, below)):
        total = add(kept.at[1 + k], got.at[1 + k])
        out[0] = total[:n]
        out[1] = total[n:]
    own[0] = add(kept.at[3], got.at[3])


def cut(kept, got, *earlier):
    n = FEAT // 2
    shapes = [(n, HALF)] * 2 + [(2, n, HALF)] * 2 + [(1, FEAT, HALF)]
    return call(cut_kernel, [], [kept, got], shapes, kept.size, earlier)


def local(tokens, cotangent, expert_ids, combine, w_gate, w_up, w_down):
    ids, weight = expert_ids.T, combine.reshape(1, -1)

    sel = select(ids, weight, tokens, cotangent)
    zhi, up0, down0 = to_zhi(sel), to_y(sel, -1), to_y(sel, 1)
    far0, down1 = to_y(down0, 1), to_zhi(down0)
    up1 = to_y(zhi, -1)
    w_gate, w_up, w_down, there = stage([w_gate, w_up, w_down], up0, zhi)
    four = pack(up0, down0, sel, zhi, earlier=[there])
    x_far1 = split(0, up1, there)
    three = pack(far0, up1, down1, earlier=[x_far1])
    d_far1 = split(1, down1, x_far1)
    first = gate_first(four, three, w_gate, w_up, d_far1)
    x_far1, d_far1 = to_y(x_far1, -1), to_y(d_far1, 1)
    four_other, three_other = to_core(four), to_core(three)
    far1 = pair(x_far1, d_far1)
    parts = [four, three, far1, four_other, three_other, to_core(far1)]
    hidden, act, slope = gate_last(x_far1, w_gate, w_up, first, four_other, three_other)
    d_rows, d_sent = back_other(four, three, d_far1, w_down, hidden, act, slope)
    d_got = to_core(d_sent)
    d_mine = back_own(d_rows, w_down, act, slope)

    far_a, far_b = gate_up_grads([(2, None)], parts, d_mine, d_got)
    far_got_a, far_got_b = lax.optimization_barrier((to_x(far_a, 1), to_x(far_b, -1)))
    down_kept, down_sent = down_grads(parts, hidden, d_got, far_a)
    down_got = to_zlo(down_sent)
    out = out_terms(hidden, w_down, down_kept)
    row_far_a, row_far_b, row_above, row_below, row_own = row_terms(
        d_mine, d_sent, w_gate, w_up, out
    )
    row_got_a, row_got_b = to_y(row_far_a, 1), to_y(row_far_b, -1)
    above1, below1 = gate_up_grads([(1, 1), (3, 1)], parts, d_mine, d_got, row_own)
    (below1,) = add_pairs(below1, far_got_b)
    above1 = after(above1, below1)
    above0, below0, own0, own1 = gate_up_grads(
        [(1, 0), (3, 0), (0, None)], parts, d_mine, d_got, below1
    )
    above1, below1 = to_x(above1, 1), to_x(below1, -1)
    (above0,) = add_pairs(above0, far_got_a)
    row_above, row_below = add_into(row_above, row_got_a, row_below, row_got_b, above0)
    row_above, row_below = to_y(row_above, 1), to_y(row_below, -1)
    sum1 = add_all(own1, above1, below1)
    far_a, far_b, above, below, down_own = cut(down_kept, down_got, sum1)
    above0, below0, *_ = lax.optimization_barrier((above0, below0, above1, below1, down_got))
    above0, below0 = to_x(above0, 1), to_x(below0, -1)
    sum1 = to_zlo(sum1)
    far_a, far_b = to_x(far_a, 1), to_x(far_b, -1)
    row_kept, row_sent = add_three(row_own, row_above, row_below)
    row_got = to_zhi(row_sent)
    expert_output, token_grad = place_rows(ids, weight, row_kept, row_got)
    mine, theirs = halves(own0, above0, below0, sum1)
    gate_grad, up_grad = join(mine, to_core(theirs))
    above, below = add_into(above, far_a, below, far_b)
    whole = lambda v: v.reshape(1, FEAT, HALF)
    above, below = whole(to_x(above, 1)), whole(to_x(below, -1))
    mine, theirs = halves(down_own, above, below)
    (down_grad,) = join(mine, to_core(theirs))
    return (expert_output, token_grad, gate_grad, up_grad, down_grad.T)


def solution(mesh):
    placed = (
        P(("dp", "tensor"), None),
        P(("dp", "tensor"), None),
        P(("dp", "tensor"), None),
        P(("dp", "tensor")),
        P(None, "tensor"),
        P(None, "tensor"),
        P("tensor", None),
    )
    return jax.shard_map(
        local,
        mesh=mesh,
        in_specs=placed,
        out_specs=(
            P(("dp", "tensor"), None),
            P(("dp", "tensor"), None),
            P("dp", "tensor"),
            P("dp", "tensor"),
            P("tensor", "dp"),
        ),
        check_vma=False,
    )
```

```python
import functools
import itertools
import math

import jax
import jax.numpy as jnp
from jax import lax
from jax.experimental import pallas as pl
from jax.experimental.pallas import tpu as pltpu
from jax.sharding import PartitionSpec as P

SLOTS = 48
ROWS = 384
DW = 3072
FF = 1024
HALF = 512
FEAT = 384
BF = jnp.bfloat16
F32 = jnp.float32
VMEM = 10 * 1024 * 1024
COST = 1000

IN_VMEM = pl.BlockSpec(memory_space=pltpu.VMEM)
IN_SMEM = pl.BlockSpec(memory_space=pltpu.SMEM)
IN_HBM = pl.BlockSpec(memory_space=pltpu.HBM)

DIM = (4, 2, 2, 2, 4)


def linear(place):
    r = 0
    for q, n in zip(place, DIM):
        r = r * n + q % n
    return r


def shift(value, axis, by):
    pairs = []
    for place in itertools.product(*map(range, DIM)):
        to = list(place)
        to[axis] += by
        pairs.append((linear(place), linear(to)))
    return lax.ppermute(value, ("dp", "tensor"), pairs)


to_x = lambda v, by: shift(v, 0, by)
to_zlo = lambda v: shift(v, 1, 1)
to_core = lambda v: shift(v, 2, 1)
to_zhi = lambda v: shift(v, 3, 1)
to_y = lambda v, by: shift(v, 4, by)


def dot(a, b):
    return jnp.dot(a, b, preferred_element_type=F32)


def dot_t(a, b):
    return lax.dot_general(a, b, (((1,), (1,)), ((), ())), preferred_element_type=F32)


def t_dot(a, b):
    return lax.dot_general(a, b, (((0,), (0,)), ((), ())), preferred_element_type=F32)


def cost(flops, nbytes):
    return pl.CostEstimate(flops=int(flops / COST), bytes_accessed=int(nbytes / COST), transcendentals=0)


def params():
    return pltpu.CompilerParams(vmem_limit_bytes=VMEM)


def after(value, *others):
    return lax.optimization_barrier((value, *others))[0]


def picks_of(ids, weight):
    n = ids.shape[1]
    chosen = (ids[0:1] == 0) | (ids[1:2] == 0)
    ones = jnp.where(chosen, 1.0, 0.0).astype(BF)
    before = lax.broadcasted_iota(jnp.int32, (n, n), 0) <= lax.broadcasted_iota(jnp.int32, (n, n), 1)
    place = dot(jnp.broadcast_to(ones, (8, n)), jnp.where(before, 1.0, 0.0).astype(BF))[0:1]
    place = place.astype(jnp.int32) - 1
    slot = lax.broadcasted_iota(jnp.int32, (SLOTS, n), 0)
    picks = jnp.where((place == slot) & chosen, 1.0, 0.0)
    return picks.astype(BF), jnp.sum(picks * weight, axis=1, keepdims=True)


def select_kernel(ids, weight, x, d, out, ids_here, weight_here, x_here, d_here, sems):
    copies = [
        pltpu.make_async_copy(far, near, sems.at[k])
        for k, (far, near) in enumerate(
            ((ids, ids_here), (weight, weight_here), (x, x_here), (d, d_here))
        )
    ]
    for copy in copies:
        copy.start()
    copies[0].wait()
    copies[1].wait()
    picks, slot_weight = picks_of(ids_here[...], weight_here[...])
    copies[2].wait()
    out[0] = dot(picks, x_here[...]).astype(BF)
    copies[3].wait()
    out[1] = (dot(picks, d_here[...]) * slot_weight).astype(BF)


def in_hbm(array):
    return pltpu.with_memory_space_constraint(array, pltpu.HBM)


def select(*arrays):
    return pl.pallas_call(
        select_kernel,
        in_specs=[IN_HBM] * 4,
        out_specs=IN_VMEM,
        out_shape=pltpu.VMEM((2, SLOTS, DW), BF),
        scratch_shapes=[pltpu.VMEM(a.shape, a.dtype) for a in arrays]
        + [pltpu.SemaphoreType.DMA((4,))],
        compiler_params=params(),
        cost_estimate=cost(4 * SLOTS * 128 * DW, 2.2e6),
    )(*map(in_hbm, arrays))


def place_kernel(ids, weight, kept, got, output, token_grad):
    picks, slot_weight = picks_of(ids[...], weight[...])
    out = kept[0].astype(F32) + got[0].astype(F32)
    output[...] = t_dot(picks, (out * slot_weight).astype(BF)).astype(BF)
    back = kept[1].astype(F32) + got[1].astype(F32)
    token_grad[...] = t_dot(picks, back.astype(BF)).astype(BF)


def place_rows(ids, weight, kept, got):
    return pl.pallas_call(
        place_kernel,
        in_specs=[IN_VMEM] * 4,
        out_specs=[IN_VMEM] * 2,
        out_shape=[jax.ShapeDtypeStruct((128, DW), BF)] * 2,
        compiler_params=params(),
        cost_estimate=cost(4 * SLOTS * 128 * DW, 2.8e6),
    )(ids, weight, kept, got)


IN_ANY = pl.BlockSpec(memory_space=pl.ANY)


def without(first, count, kernel):
    def run(*refs):
        kernel(*refs[:first], *refs[first + count :])

    return run


def call(kernel, scalars, arrays, shapes, flops, earlier=(), hbm=(), scratch=(), aliases=None):
    shapes = [s if isinstance(s[0], tuple) else (s, BF) for s in shapes]
    size = sum(a.size for a in arrays) + sum(math.prod(s) for s, _ in shapes)
    inputs = len(scalars) + len(arrays) + len(hbm)
    return pl.pallas_call(
        without(inputs, len(earlier), kernel),
        in_specs=[IN_SMEM] * len(scalars)
        + [IN_VMEM] * len(arrays)
        + [IN_HBM] * len(hbm)
        + [IN_ANY] * len(earlier),
        out_specs=[IN_VMEM] * len(shapes),
        out_shape=[pltpu.VMEM(s, t) for s, t in shapes],
        scratch_shapes=list(scratch),
        input_output_aliases=aliases or {},
        compiler_params=params(),
        cost_estimate=cost(flops, size),
    )(*scalars, *arrays, *map(in_hbm, hbm), *earlier)


def stage_kernel(n, *refs):
    *refs, token, sems = refs
    copies = [pltpu.make_async_copy(refs[i], refs[n + i], sems.at[i]) for i in range(n)]
    for copy in copies:
        copy.start()
    token[...] = jnp.zeros_like(token)
    for copy in copies:
        copy.wait()


def stage(arrays, *earlier):
    return call(
        functools.partial(stage_kernel, len(arrays)),
        [],
        [],
        [a.shape for a in arrays] + [((8, 128), F32)],
        1,
        earlier,
        hbm=arrays,
        scratch=[pltpu.SemaphoreType.DMA((len(arrays),))],
    )


def place_of():
    dp = lax.axis_index("dp")
    return dp % 2, (dp // 2) % 2, dp // 4


def half(h):
    return pl.ds(pl.multiple_of(h * HALF, HALF), HALF)


def pack_kernel(*refs):
    *chunks, out = refs
    for k, chunk in enumerate(chunks):
        out[:, k * SLOTS : (k + 1) * SLOTS] = chunk[...]


def pack(*chunks, earlier=()):
    return call(pack_kernel, [], chunks, [(2, SLOTS * len(chunks), DW)], 1, earlier)[0]


def pair_kernel(x, d, out):
    out[0] = x[...]
    out[1] = d[...]


def pair(x, d):
    return call(pair_kernel, [], [x, d], [(2, SLOTS, DW)], 1)[0]


def split_kernel(which, chunk, out):
    out[...] = chunk[which]


def split(which, chunk, *earlier):
    kernel = functools.partial(split_kernel, which)
    return call(kernel, [], [chunk], [(SLOTS, DW)], 1, earlier)[0]


FIRST = ROWS - SLOTS


def gate_rows(r, rows, w_gate, w_up, hidden, act, slope):
    for h in range(2):
        at = slice(h * HALF, (h + 1) * HALF)
        gate = dot(rows[...], w_gate[:, at])
        up = dot(rows[...], w_up[:, at])
        s = jax.nn.sigmoid(gate)
        silu = gate * s
        act[r, at] = silu
        slope[r, at] = up * s * (1.0 + gate * (1.0 - s))
        hidden[r, at] = (silu * up).astype(BF)


GATE_SHAPES = [(ROWS, FF), ((ROWS, FF), F32), ((ROWS, FF), F32)]


def gate_first_kernel(a, b, w_gate, w_up, hidden, act, slope, rows):
    n = a.shape[1]
    rows[:n] = a[0]
    rows[n:] = b[0]
    gate_rows(slice(0, FIRST), rows, w_gate, w_up, hidden, act, slope)


def gate_first(a, b, w_gate, w_up, *earlier):
    return call(
        gate_first_kernel,
        [],
        [a, b, w_gate, w_up],
        GATE_SHAPES,
        4 * FIRST * DW * FF,
        earlier,
        scratch=[pltpu.VMEM((FIRST, DW), BF)],
    )


def gate_last_kernel(chunk, w_gate, w_up, *refs):
    hidden, act, slope = refs[3:]
    gate_rows(slice(FIRST, ROWS), chunk, w_gate, w_up, hidden, act, slope)


def gate_last(chunk, w_gate, w_up, first, *earlier):
    return call(
        gate_last_kernel,
        [],
        [chunk, w_gate, w_up, *first],
        GATE_SHAPES,
        4 * SLOTS * DW * FF,
        earlier,
        aliases={3 + k: k for k in range(3)},
    )


def back_half(mine, rows, w_down, act, slope, out):
    at = half(mine)
    d_hidden = dot_t(rows[...], w_down[at, :])
    out[0] = (d_hidden * slope[:, at]).astype(BF)
    out[1] = (d_hidden * act[:, at]).astype(BF)


def back_other_kernel(a, b, last, w_down, hidden, act, slope, rows, out):
    n = a.shape[1]
    rows[:n] = a[1]
    rows[n:FIRST] = b[1]
    rows[FIRST:] = last[...]
    other = 1 - place_of()[0]
    out[2] = hidden[:, half(other)]
    back_half(other, rows, w_down, act, slope, out)


def back_other(a, b, last, w_down, hidden, act, slope, *earlier):
    arrays = [a, b, last, w_down, hidden, act, slope]
    shapes = [(ROWS, DW), (3, ROWS, HALF)]
    return call(back_other_kernel, [], arrays, shapes, ROWS * DW * FF, earlier)


def back_own_kernel(rows, w_down, act, slope, out):
    back_half(place_of()[0], rows, w_down, act, slope, out)


def back_own(rows, w_down, act, slope):
    shapes = [(2, ROWS, HALF)]
    return call(back_own_kernel, [], [rows, w_down, act, slope], shapes, ROWS * DW * FF)[0]


def out_kernel(hidden, w_down, out):
    for j in range(0, DW, 768):
        at = slice(j, j + 768)
        out[:, at] = dot(hidden[...], w_down[:, at]).astype(BF)


def out_terms(hidden, w_down, *earlier):
    return call(out_kernel, [], [hidden, w_down], [(ROWS, DW)], 2 * ROWS * DW * FF, earlier)[0]


def token_kernel(mine, other, w_gate, w_up, out, far_a, far_b, above, below, own):
    targets = [above.at[0], below.at[0], own.at[0], own.at[1], far_a, above.at[1], below.at[1], far_b]
    core = place_of()[0]
    for j in range(0, DW, 768):
        at = slice(j, j + 768)
        back = sum(
            dot_t(d[m], w[at, half(h)])
            for d, h in ((mine, core), (other, 1 - core))
            for m, w in enumerate((w_gate, w_up))
        )
        for k, target in enumerate(targets):
            rows = slice(k * SLOTS, (k + 1) * SLOTS)
            target[0, :, at] = out[rows, at]
            target[1, :, at] = back[rows].astype(BF)


def row_terms(mine, other, w_gate, w_up, out, *earlier):
    shapes = [(2, SLOTS, DW)] * 2 + [(2, 2, SLOTS, DW)] * 3
    return call(
        token_kernel, [], [mine, other, w_gate, w_up, out], shapes, 4 * ROWS * DW * FF, earlier
    )


def both(*rows):
    return jnp.concatenate(rows, axis=0)


def features(place, dx):
    at = ((place[2] + dx) % 4) * (2 * FEAT)
    return pl.ds(pl.multiple_of(at, 2 * FEAT), 2 * FEAT)


def store_pair(place, first, second, low, high):
    @pl.when(place[1] == 0)
    def _():
        first[...] = low
        second[...] = high

    @pl.when(place[1] == 1)
    def _():
        first[...] = high
        second[...] = low


def rows_at(which, parts, at):
    return both(*(p[which, :, at] for p in parts))


def grads_kernel(pairs, *refs):
    x_parts, (mine, got, *outs) = refs[:6], refs[6:]
    place = place_of()
    terms = [both(mine[m], got[m]) for m in range(2)]
    for dx, dz in pairs:
        if dz is None:
            at = features(place, dx)
        else:
            at = ((place[2] + dx) % 4) * (2 * FEAT) + ((place[1] + dz) % 2) * FEAT
            at = pl.ds(pl.multiple_of(at, FEAT), FEAT)
        x = rows_at(0, x_parts, at)
        here = [outs.pop(0) for _ in range(2 if dz is None else 1)]
        for m in range(2):
            result = t_dot(x, terms[m]).astype(BF)
            if dz is None:
                store_pair(place, here[0].at[m], here[1].at[m], result[:FEAT], result[FEAT:])
            else:
                here[0][m] = result


def gate_up_grads(pairs, x_parts, mine, got, *earlier):
    n = sum(2 if dz is None else 1 for _, dz in pairs)
    return call(
        functools.partial(grads_kernel, pairs),
        [],
        [*x_parts, mine, got],
        [(2, FEAT, HALF)] * n,
        n * ROWS * DW * FF / 2,
        earlier,
    )


def down_kernel(*refs):
    d_parts, (hidden, got, kept, sent) = refs[:6], refs[6:]
    place = place_of()
    h = both(hidden[:, half(place[0])], got[2])
    for k, dx in enumerate((2, 1, 3, 0)):
        at = features(place, dx)
        result = t_dot(rows_at(1, d_parts, at), h).astype(BF)
        store_pair(place, kept.at[k], sent.at[k], result[:FEAT], result[FEAT:])


def down_grads(parts, hidden, got, *earlier):
    shapes = [(4, FEAT, HALF)] * 2
    return call(down_kernel, [], [*parts, hidden, got], shapes, 2 * ROWS * DW * FF, earlier)


def add(*terms):
    return sum(t[...].astype(F32) for t in terms).astype(BF)


def add_pairs_kernel(n, *refs):
    for k in range(n):
        refs[2 * n + k][...] = add(refs[2 * k], refs[2 * k + 1])


def add_pairs(*terms):
    n = len(terms) // 2
    shapes = [t.shape for t in terms[::2]]
    flops = sum(math.prod(s) for s in shapes)
    return call(functools.partial(add_pairs_kernel, n), [], terms, shapes, flops)


def add_all_kernel(*refs):
    refs[-1][...] = add(*refs[:-1])


def add_all(*terms):
    return call(add_all_kernel, [], terms, [terms[0].shape], 2 * terms[0].size)[0]


def add_into_kernel(above, got_a, below, got_b, new_above, new_below):
    new_above[0] = add(above.at[0], got_a)
    new_above[1] = above[1]
    new_below[0] = below[0]
    new_below[1] = add(below.at[1], got_b)


def add_into(above, got_a, below, got_b, *earlier):
    return call(
        add_into_kernel, [], [above, got_a, below, got_b], [above.shape] * 2, above.size, earlier
    )


def add_three_kernel(own, above, below, kept, sent):
    kept[...] = add(own.at[0], above.at[0], below.at[0])
    sent[...] = add(own.at[1], above.at[1], below.at[1])


def add_three(own, above, below):
    return call(add_three_kernel, [], [own, above, below], [own.shape[1:]] * 2, 2 * own.size)


def halves_kernel(*refs):
    *terms, mine, theirs = refs
    place = place_of()
    total = add(*terms)
    low, high = total[:, : FEAT // 2], total[:, FEAT // 2 :]

    @pl.when(place[0] == 0)
    def _():
        mine[...] = low
        theirs[...] = high

    @pl.when(place[0] == 1)
    def _():
        mine[...] = high
        theirs[...] = low


def halves(*terms):
    n = terms[0].shape[0]
    return call(halves_kernel, [], terms, [(n, FEAT // 2, HALF)] * 2, 2 * terms[0].size)


def join_kernel(mine, got, *outs):
    place = place_of()
    for k, out in enumerate(outs):

        @pl.when(place[0] == 0)
        def _():
            out[:, :HALF] = mine[k]
            out[:, HALF:] = got[k]

        @pl.when(place[0] == 1)
        def _():
            out[:, :HALF] = got[k]
            out[:, HALF:] = mine[k]


def join(mine, got):
    n = mine.shape[0]
    return pl.pallas_call(
        join_kernel,
        in_specs=[IN_VMEM, IN_VMEM],
        out_specs=[IN_VMEM] * n,
        out_shape=[jax.ShapeDtypeStruct((FEAT // 2, FF), BF)] * n,
        compiler_params=params(),
        cost_estimate=cost(mine.size, 8 * mine.size),
    )(mine, got)


def cut_kernel(kept, got, far_a, far_b, above, below, own):
    n = FEAT // 2
    far = add(kept.at[0], got.at[0])
    far_a[...] = far[:n]
    far_b[...] = far[n:]
    for k, out in enumerate((above, below)):
        total = add(kept.at[1 + k], got.at[1 + k])
        out[0] = total[:n]
        out[1] = total[n:]
    own[0] = add(kept.at[3], got.at[3])


def cut(kept, got, *earlier):
    n = FEAT // 2
    shapes = [(n, HALF)] * 2 + [(2, n, HALF)] * 2 + [(1, FEAT, HALF)]
    return call(cut_kernel, [], [kept, got], shapes, kept.size, earlier)


def local(tokens, cotangent, expert_ids, combine, w_gate, w_up, w_down):
    ids, weight = expert_ids.T, combine.reshape(1, -1)

    sel = select(ids, weight, tokens, cotangent)
    zhi, up0, down0 = to_zhi(sel), to_y(sel, -1), to_y(sel, 1)
    far0, down1 = to_y(down0, 1), to_zhi(down0)
    up1 = to_y(zhi, -1)
    w_gate, w_up, w_down, there = stage([w_gate, w_up, w_down], up0, zhi)
    four = pack(up0, down0, sel, zhi, earlier=[there])
    x_far1 = split(0, up1, there)
    three = pack(far0, up1, down1, earlier=[x_far1])
    d_far1 = split(1, down1, x_far1)
    first = gate_first(four, three, w_gate, w_up, d_far1)
    x_far1, d_far1 = to_y(x_far1, -1), to_y(d_far1, 1)
    four_other, three_other = to_core(four), to_core(three)
    far1 = pair(x_far1, d_far1)
    parts = [four, three, far1, four_other, three_other, to_core(far1)]
    hidden, act, slope = gate_last(x_far1, w_gate, w_up, first, four_other, three_other)
    d_rows, d_sent = back_other(four, three, d_far1, w_down, hidden, act, slope, far1)
    d_got = to_core(d_sent)
    d_mine = back_own(d_rows, w_down, act, slope)

    far_a, far_b = gate_up_grads([(2, None)], parts, d_mine, d_got)
    far_got_a, far_got_b = lax.optimization_barrier((to_x(far_a, 1), to_x(far_b, -1)))
    down_kept, down_sent = down_grads(parts, hidden, d_got, far_a)
    down_got = to_zlo(down_sent)
    out = out_terms(hidden, w_down, down_kept)
    row_far_a, row_far_b, row_above, row_below, row_own = row_terms(
        d_mine, d_sent, w_gate, w_up, out
    )
    row_got_a, row_got_b = to_y(row_far_a, 1), to_y(row_far_b, -1)
    above1, below1 = gate_up_grads([(1, 1), (3, 1)], parts, d_mine, d_got, row_own)
    (below1,) = add_pairs(below1, far_got_b)
    above1 = after(above1, below1)
    above0, below0, own0, own1 = gate_up_grads(
        [(1, 0), (3, 0), (0, None)], parts, d_mine, d_got, below1
    )
    above1, below1 = to_x(above1, 1), to_x(below1, -1)
    (above0,) = add_pairs(above0, far_got_a)
    row_above, row_below = add_into(row_above, row_got_a, row_below, row_got_b, above0)
    row_above, row_below = to_y(row_above, 1), to_y(row_below, -1)
    sum1 = add_all(own1, above1, below1)
    far_a, far_b, above, below, down_own = cut(down_kept, down_got, sum1)
    above0, below0, *_ = lax.optimization_barrier((above0, below0, above1, below1, down_got))
    above0, below0 = to_x(above0, 1), to_x(below0, -1)
    sum1 = to_zlo(sum1)
    far_a, far_b = to_x(far_a, 1), to_x(far_b, -1)
    row_kept, row_sent = add_three(row_own, row_above, row_below)
    row_got = to_zhi(row_sent)
    expert_output, token_grad = place_rows(ids, weight, row_kept, row_got)
    mine, theirs = halves(own0, above0, below0, sum1)
    gate_grad, up_grad = join(mine, to_core(theirs))
    above, below = add_into(above, far_a, below, far_b)
    whole = lambda v: v.reshape(1, FEAT, HALF)
    above, below = whole(to_x(above, 1)), whole(to_x(below, -1))
    mine, theirs = halves(down_own, above, below)
    (down_grad,) = join(mine, to_core(theirs))
    return (expert_output, token_grad, gate_grad, up_grad, down_grad.T)


def solution(mesh):
    placed = (
        P(("dp", "tensor"), None),
        P(("dp", "tensor"), None),
        P(("dp", "tensor"), None),
        P(("dp", "tensor")),
        P(None, "tensor"),
        P(None, "tensor"),
        P("tensor", None),
    )
    return jax.shard_map(
        local,
        mesh=mesh,
        in_specs=placed,
        out_specs=(
            P(("dp", "tensor"), None),
            P(("dp", "tensor"), None),
            P("dp", "tensor"),
            P("dp", "tensor"),
            P("tensor", "dp"),
        ),
        check_vma=False,
    )
```

```python
import functools
import itertools
import math

import jax
import jax.numpy as jnp
from jax import lax
from jax.experimental import pallas as pl
from jax.experimental.pallas import tpu as pltpu
from jax.sharding import PartitionSpec as P

SLOTS = 48
ROWS = 384
DW = 3072
FF = 1024
HALF = 512
FEAT = 384
BF = jnp.bfloat16
F32 = jnp.float32
VMEM = 10 * 1024 * 1024
COST = 1000

IN_VMEM = pl.BlockSpec(memory_space=pltpu.VMEM)
IN_SMEM = pl.BlockSpec(memory_space=pltpu.SMEM)
IN_HBM = pl.BlockSpec(memory_space=pltpu.HBM)

DIM = (4, 2, 2, 2, 4)


def linear(place):
    r = 0
    for q, n in zip(place, DIM):
        r = r * n + q % n
    return r


def shift(value, axis, by):
    pairs = []
    for place in itertools.product(*map(range, DIM)):
        to = list(place)
        to[axis] += by
        pairs.append((linear(place), linear(to)))
    return lax.ppermute(value, ("dp", "tensor"), pairs)


to_x = lambda v, by: shift(v, 0, by)
to_zlo = lambda v: shift(v, 1, 1)
to_core = lambda v: shift(v, 2, 1)
to_zhi = lambda v: shift(v, 3, 1)
to_y = lambda v, by: shift(v, 4, by)


def dot(a, b):
    return jnp.dot(a, b, preferred_element_type=F32)


def dot_t(a, b):
    return lax.dot_general(a, b, (((1,), (1,)), ((), ())), preferred_element_type=F32)


def t_dot(a, b):
    return lax.dot_general(a, b, (((0,), (0,)), ((), ())), preferred_element_type=F32)


def cost(flops, nbytes):
    return pl.CostEstimate(flops=int(flops / COST), bytes_accessed=int(nbytes / COST), transcendentals=0)


def params():
    return pltpu.CompilerParams(vmem_limit_bytes=VMEM)


def after(value, *others):
    return lax.optimization_barrier((value, *others))[0]


def picks_of(ids, weight):
    n = ids.shape[1]
    chosen = (ids[0:1] == 0) | (ids[1:2] == 0)
    ones = jnp.where(chosen, 1.0, 0.0).astype(BF)
    before = lax.broadcasted_iota(jnp.int32, (n, n), 0) <= lax.broadcasted_iota(jnp.int32, (n, n), 1)
    place = dot(jnp.broadcast_to(ones, (8, n)), jnp.where(before, 1.0, 0.0).astype(BF))[0:1]
    place = place.astype(jnp.int32) - 1
    slot = lax.broadcasted_iota(jnp.int32, (SLOTS, n), 0)
    picks = jnp.where((place == slot) & chosen, 1.0, 0.0)
    return picks.astype(BF), jnp.sum(picks * weight, axis=1, keepdims=True)


def select_kernel(ids, weight, x, d, out, ids_here, weight_here, x_here, d_here, sems):
    copies = [
        pltpu.make_async_copy(far, near, sems.at[k])
        for k, (far, near) in enumerate(
            ((ids, ids_here), (weight, weight_here), (x, x_here), (d, d_here))
        )
    ]
    for copy in copies:
        copy.start()
    copies[0].wait()
    copies[1].wait()
    picks, slot_weight = picks_of(ids_here[...], weight_here[...])
    copies[2].wait()
    out[0] = dot(picks, x_here[...]).astype(BF)
    copies[3].wait()
    out[1] = (dot(picks, d_here[...]) * slot_weight).astype(BF)


def in_hbm(array):
    return pltpu.with_memory_space_constraint(array, pltpu.HBM)


def select(*arrays):
    return pl.pallas_call(
        select_kernel,
        in_specs=[IN_HBM] * 4,
        out_specs=IN_VMEM,
        out_shape=pltpu.VMEM((2, SLOTS, DW), BF),
        scratch_shapes=[pltpu.VMEM(a.shape, a.dtype) for a in arrays]
        + [pltpu.SemaphoreType.DMA((4,))],
        compiler_params=params(),
        cost_estimate=cost(4 * SLOTS * 128 * DW, 2.2e6),
    )(*map(in_hbm, arrays))


def place_kernel(ids, weight, kept, got, output, token_grad):
    picks, slot_weight = picks_of(ids[...], weight[...])
    out = kept[0].astype(F32) + got[0].astype(F32)
    output[...] = t_dot(picks, (out * slot_weight).astype(BF)).astype(BF)
    back = kept[1].astype(F32) + got[1].astype(F32)
    token_grad[...] = t_dot(picks, back.astype(BF)).astype(BF)


def place_rows(ids, weight, kept, got):
    return pl.pallas_call(
        place_kernel,
        in_specs=[IN_VMEM] * 4,
        out_specs=[IN_VMEM] * 2,
        out_shape=[jax.ShapeDtypeStruct((128, DW), BF)] * 2,
        compiler_params=params(),
        cost_estimate=cost(4 * SLOTS * 128 * DW, 2.8e6),
    )(ids, weight, kept, got)


IN_ANY = pl.BlockSpec(memory_space=pl.ANY)


def without(first, count, kernel):
    def run(*refs):
        kernel(*refs[:first], *refs[first + count :])

    return run


def call(kernel, scalars, arrays, shapes, flops, earlier=(), hbm=(), scratch=(), aliases=None):
    shapes = [s if isinstance(s[0], tuple) else (s, BF) for s in shapes]
    size = sum(a.size for a in arrays) + sum(math.prod(s) for s, _ in shapes)
    inputs = len(scalars) + len(arrays) + len(hbm)
    return pl.pallas_call(
        without(inputs, len(earlier), kernel),
        in_specs=[IN_SMEM] * len(scalars)
        + [IN_VMEM] * len(arrays)
        + [IN_HBM] * len(hbm)
        + [IN_ANY] * len(earlier),
        out_specs=[IN_VMEM] * len(shapes),
        out_shape=[pltpu.VMEM(s, t) for s, t in shapes],
        scratch_shapes=list(scratch),
        input_output_aliases=aliases or {},
        compiler_params=params(),
        cost_estimate=cost(flops, size),
    )(*scalars, *arrays, *map(in_hbm, hbm), *earlier)


def stage_kernel(n, *refs):
    *refs, token, sems = refs
    copies = [pltpu.make_async_copy(refs[i], refs[n + i], sems.at[i]) for i in range(n)]
    for copy in copies:
        copy.start()
    token[...] = jnp.zeros_like(token)
    for copy in copies:
        copy.wait()


def stage(arrays, *earlier):
    return call(
        functools.partial(stage_kernel, len(arrays)),
        [],
        [],
        [a.shape for a in arrays] + [((8, 128), F32)],
        1,
        earlier,
        hbm=arrays,
        scratch=[pltpu.SemaphoreType.DMA((len(arrays),))],
    )


def place_of():
    dp = lax.axis_index("dp")
    return dp % 2, (dp // 2) % 2, dp // 4


def half(h):
    return pl.ds(pl.multiple_of(h * HALF, HALF), HALF)


def pack_kernel(*refs):
    *chunks, out = refs
    for k, chunk in enumerate(chunks):
        out[:, k * SLOTS : (k + 1) * SLOTS] = chunk[...]


def pack(*chunks, earlier=()):
    return call(pack_kernel, [], chunks, [(2, SLOTS * len(chunks), DW)], 1, earlier)[0]


def pair_kernel(x, d, out):
    out[0] = x[...]
    out[1] = d[...]


def pair(x, d):
    return call(pair_kernel, [], [x, d], [(2, SLOTS, DW)], 1)[0]


def split_kernel(which, chunk, out):
    out[...] = chunk[which]


def split(which, chunk, *earlier):
    kernel = functools.partial(split_kernel, which)
    return call(kernel, [], [chunk], [(SLOTS, DW)], 1, earlier)[0]


FIRST = ROWS - SLOTS


def gate_rows(r, rows, w_gate, w_up, hidden, act, slope):
    for h in range(2):
        at = slice(h * HALF, (h + 1) * HALF)
        gate = dot(rows[...], w_gate[:, at])
        up = dot(rows[...], w_up[:, at])
        s = jax.nn.sigmoid(gate)
        silu = gate * s
        act[r, at] = silu
        slope[r, at] = up * s * (1.0 + gate * (1.0 - s))
        hidden[r, at] = (silu * up).astype(BF)


GATE_SHAPES = [(ROWS, FF), ((ROWS, FF), F32), ((ROWS, FF), F32)]


def gate_first_kernel(a, b, w_gate, w_up, hidden, act, slope, rows):
    n = a.shape[1]
    rows[:n] = a[0]
    rows[n:] = b[0]
    gate_rows(slice(0, FIRST), rows, w_gate, w_up, hidden, act, slope)


def gate_first(a, b, w_gate, w_up, *earlier):
    return call(
        gate_first_kernel,
        [],
        [a, b, w_gate, w_up],
        GATE_SHAPES,
        4 * FIRST * DW * FF,
        earlier,
        scratch=[pltpu.VMEM((FIRST, DW), BF)],
    )


def gate_last_kernel(chunk, w_gate, w_up, *refs):
    hidden, act, slope = refs[3:]
    gate_rows(slice(FIRST, ROWS), chunk, w_gate, w_up, hidden, act, slope)


def gate_last(chunk, w_gate, w_up, first, *earlier):
    return call(
        gate_last_kernel,
        [],
        [chunk, w_gate, w_up, *first],
        GATE_SHAPES,
        4 * SLOTS * DW * FF,
        earlier,
        aliases={3 + k: k for k in range(3)},
    )


def back_half(mine, rows, w_down, act, slope, out):
    at = half(mine)
    d_hidden = dot_t(rows[...], w_down[at, :])
    out[0] = (d_hidden * slope[:, at]).astype(BF)
    out[1] = (d_hidden * act[:, at]).astype(BF)


def back_other_kernel(a, b, last, w_down, hidden, act, slope, rows, out):
    n = a.shape[1]
    rows[:n] = a[1]
    rows[n:FIRST] = b[1]
    rows[FIRST:] = last[...]
    other = 1 - place_of()[0]
    out[2] = hidden[:, half(other)]
    back_half(other, rows, w_down, act, slope, out)


def back_other(a, b, last, w_down, hidden, act, slope, *earlier):
    arrays = [a, b, last, w_down, hidden, act, slope]
    shapes = [(ROWS, DW), (3, ROWS, HALF)]
    return call(back_other_kernel, [], arrays, shapes, ROWS * DW * FF, earlier)


def back_own_kernel(rows, w_down, act, slope, out):
    back_half(place_of()[0], rows, w_down, act, slope, out)


def back_own(rows, w_down, act, slope):
    shapes = [(2, ROWS, HALF)]
    return call(back_own_kernel, [], [rows, w_down, act, slope], shapes, ROWS * DW * FF)[0]


def out_kernel(hidden, w_down, out):
    for j in range(0, DW, 768):
        at = slice(j, j + 768)
        out[:, at] = dot(hidden[...], w_down[:, at]).astype(BF)


def out_terms(hidden, w_down, *earlier):
    return call(out_kernel, [], [hidden, w_down], [(ROWS, DW)], 2 * ROWS * DW * FF, earlier)[0]


def token_kernel(mine, other, w_gate, w_up, out, far_a, far_b, above, below, own):
    targets = [above.at[0], below.at[0], own.at[0], own.at[1], far_a, above.at[1], below.at[1], far_b]
    core = place_of()[0]
    for j in range(0, DW, 768):
        at = slice(j, j + 768)
        back = sum(
            dot_t(d[m], w[at, half(h)])
            for d, h in ((mine, core), (other, 1 - core))
            for m, w in enumerate((w_gate, w_up))
        )
        for k, target in enumerate(targets):
            rows = slice(k * SLOTS, (k + 1) * SLOTS)
            target[0, :, at] = out[rows, at]
            target[1, :, at] = back[rows].astype(BF)


def row_terms(mine, other, w_gate, w_up, out, *earlier):
    shapes = [(2, SLOTS, DW)] * 2 + [(2, 2, SLOTS, DW)] * 3
    return call(
        token_kernel, [], [mine, other, w_gate, w_up, out], shapes, 4 * ROWS * DW * FF, earlier
    )


def both(*rows):
    return jnp.concatenate(rows, axis=0)


def features(place, dx):
    at = ((place[2] + dx) % 4) * (2 * FEAT)
    return pl.ds(pl.multiple_of(at, 2 * FEAT), 2 * FEAT)


def store_pair(place, first, second, low, high):
    @pl.when(place[1] == 0)
    def _():
        first[...] = low
        second[...] = high

    @pl.when(place[1] == 1)
    def _():
        first[...] = high
        second[...] = low


def rows_at(which, parts, at):
    return both(*(p[which, :, at] for p in parts))


def grads_kernel(pairs, *refs):
    x_parts, (mine, got, *outs) = refs[:6], refs[6:]
    place = place_of()
    terms = [both(mine[m], got[m]) for m in range(2)]
    for dx, dz in pairs:
        if dz is None:
            at = features(place, dx)
        else:
            at = ((place[2] + dx) % 4) * (2 * FEAT) + ((place[1] + dz) % 2) * FEAT
            at = pl.ds(pl.multiple_of(at, FEAT), FEAT)
        x = rows_at(0, x_parts, at)
        here = [outs.pop(0) for _ in range(2 if dz is None else 1)]
        for m in range(2):
            result = t_dot(x, terms[m]).astype(BF)
            if dz is None:
                store_pair(place, here[0].at[m], here[1].at[m], result[:FEAT], result[FEAT:])
            else:
                here[0][m] = result


def gate_up_grads(pairs, x_parts, mine, got, *earlier):
    n = sum(2 if dz is None else 1 for _, dz in pairs)
    return call(
        functools.partial(grads_kernel, pairs),
        [],
        [*x_parts, mine, got],
        [(2, FEAT, HALF)] * n,
        n * ROWS * DW * FF / 2,
        earlier,
    )


def down_kernel(*refs):
    d_parts, (hidden, got, kept, sent) = refs[:6], refs[6:]
    place = place_of()
    h = both(hidden[:, half(place[0])], got[2])
    for k, dx in enumerate((2, 1, 3, 0)):
        at = features(place, dx)
        result = t_dot(rows_at(1, d_parts, at), h).astype(BF)
        store_pair(place, kept.at[k], sent.at[k], result[:FEAT], result[FEAT:])


def down_grads(parts, hidden, got, *earlier):
    shapes = [(4, FEAT, HALF)] * 2
    return call(down_kernel, [], [*parts, hidden, got], shapes, 2 * ROWS * DW * FF, earlier)


def add(*terms):
    return sum(t[...].astype(F32) for t in terms).astype(BF)


def add_pairs_kernel(n, *refs):
    for k in range(n):
        refs[2 * n + k][...] = add(refs[2 * k], refs[2 * k + 1])


def add_pairs(*terms):
    n = len(terms) // 2
    shapes = [t.shape for t in terms[::2]]
    flops = sum(math.prod(s) for s in shapes)
    return call(functools.partial(add_pairs_kernel, n), [], terms, shapes, flops)


def add_all_kernel(*refs):
    refs[-1][...] = add(*refs[:-1])


def add_all(*terms):
    return call(add_all_kernel, [], terms, [terms[0].shape], 2 * terms[0].size)[0]


def add_into_kernel(above, got_a, below, got_b, new_above, new_below):
    new_above[0] = add(above.at[0], got_a)
    new_above[1] = above[1]
    new_below[0] = below[0]
    new_below[1] = add(below.at[1], got_b)


def add_into(above, got_a, below, got_b, *earlier):
    return call(
        add_into_kernel, [], [above, got_a, below, got_b], [above.shape] * 2, above.size, earlier
    )


def add_three_kernel(own, above, below, kept, sent):
    kept[...] = add(own.at[0], above.at[0], below.at[0])
    sent[...] = add(own.at[1], above.at[1], below.at[1])


def add_three(own, above, below):
    return call(add_three_kernel, [], [own, above, below], [own.shape[1:]] * 2, 2 * own.size)


def halves_kernel(*refs):
    *terms, mine, theirs = refs
    place = place_of()
    total = add(*terms)
    low, high = total[:, : FEAT // 2], total[:, FEAT // 2 :]

    @pl.when(place[0] == 0)
    def _():
        mine[...] = low
        theirs[...] = high

    @pl.when(place[0] == 1)
    def _():
        mine[...] = high
        theirs[...] = low


def halves(*terms):
    n = terms[0].shape[0]
    return call(halves_kernel, [], terms, [(n, FEAT // 2, HALF)] * 2, 2 * terms[0].size)


def join_kernel(mine, got, *outs):
    place = place_of()
    for k, out in enumerate(outs):

        @pl.when(place[0] == 0)
        def _():
            out[:, :HALF] = mine[k]
            out[:, HALF:] = got[k]

        @pl.when(place[0] == 1)
        def _():
            out[:, :HALF] = got[k]
            out[:, HALF:] = mine[k]


def join(mine, got):
    n = mine.shape[0]
    return pl.pallas_call(
        join_kernel,
        in_specs=[IN_VMEM, IN_VMEM],
        out_specs=[IN_VMEM] * n,
        out_shape=[jax.ShapeDtypeStruct((FEAT // 2, FF), BF)] * n,
        compiler_params=params(),
        cost_estimate=cost(mine.size, 8 * mine.size),
    )(mine, got)


def cut_kernel(kept, got, far_a, far_b, above, below, own):
    n = FEAT // 2
    far = add(kept.at[0], got.at[0])
    far_a[...] = far[:n]
    far_b[...] = far[n:]
    for k, out in enumerate((above, below)):
        total = add(kept.at[1 + k], got.at[1 + k])
        out[0] = total[:n]
        out[1] = total[n:]
    own[0] = add(kept.at[3], got.at[3])


def cut(kept, got, *earlier):
    n = FEAT // 2
    shapes = [(n, HALF)] * 2 + [(2, n, HALF)] * 2 + [(1, FEAT, HALF)]
    return call(cut_kernel, [], [kept, got], shapes, kept.size, earlier)


def local(tokens, cotangent, expert_ids, combine, w_gate, w_up, w_down):
    ids, weight = expert_ids.T, combine.reshape(1, -1)

    sel = select(ids, weight, tokens, cotangent)
    zhi, up0, down0 = to_zhi(sel), to_y(sel, -1), to_y(sel, 1)
    far0, down1 = to_y(down0, 1), to_zhi(down0)
    up1 = to_y(zhi, -1)
    w_gate, w_up, w_down, there = stage([w_gate, w_up, w_down], up0, zhi)
    four = pack(up0, down0, sel, zhi, earlier=[there])
    x_far1 = split(0, up1, there)
    d_far1 = split(1, down1, x_far1)
    three = pack(far0, up1, down1, earlier=[d_far1])
    first = gate_first(four, three, w_gate, w_up, d_far1)
    x_far1, d_far1 = to_y(x_far1, -1), to_y(d_far1, 1)
    four_other, three_other = to_core(four), to_core(three)
    far1 = pair(x_far1, d_far1)
    parts = [four, three, far1, four_other, three_other, to_core(far1)]
    hidden, act, slope = gate_last(x_far1, w_gate, w_up, first, four_other, three_other)
    d_rows, d_sent = back_other(four, three, d_far1, w_down, hidden, act, slope, far1)
    d_got = to_core(d_sent)
    d_mine = back_own(d_rows, w_down, act, slope)

    far_a, far_b = gate_up_grads([(2, None)], parts, d_mine, d_got)
    far_got_a, far_got_b = lax.optimization_barrier((to_x(far_a, 1), to_x(far_b, -1)))
    down_kept, down_sent = down_grads(parts, hidden, d_got, far_a)
    down_got = to_zlo(down_sent)
    out = out_terms(hidden, w_down, down_kept)
    row_far_a, row_far_b, row_above, row_below, row_own = row_terms(
        d_mine, d_sent, w_gate, w_up, out
    )
    row_got_a, row_got_b = to_y(row_far_a, 1), to_y(row_far_b, -1)
    above1, below1 = gate_up_grads([(1, 1), (3, 1)], parts, d_mine, d_got, row_own)
    (below1,) = add_pairs(below1, far_got_b)
    above1 = after(above1, below1)
    above0, below0, own0, own1 = gate_up_grads(
        [(1, 0), (3, 0), (0, None)], parts, d_mine, d_got, below1
    )
    above1, below1 = to_x(above1, 1), to_x(below1, -1)
    (above0,) = add_pairs(above0, far_got_a)
    row_above, row_below = add_into(row_above, row_got_a, row_below, row_got_b, above0)
    row_above, row_below = to_y(row_above, 1), to_y(row_below, -1)
    sum1 = add_all(own1, above1, below1)
    far_a, far_b, above, below, down_own = cut(down_kept, down_got, sum1)
    above0, below0, *_ = lax.optimization_barrier((above0, below0, above1, below1, down_got))
    above0, below0 = to_x(above0, 1), to_x(below0, -1)
    sum1 = to_zlo(sum1)
    far_a, far_b = to_x(far_a, 1), to_x(far_b, -1)
    row_kept, row_sent = add_three(row_own, row_above, row_below)
    row_got = to_zhi(row_sent)
    expert_output, token_grad = place_rows(ids, weight, row_kept, row_got)
    mine, theirs = halves(own0, above0, below0, sum1)
    gate_grad, up_grad = join(mine, to_core(theirs))
    above, below = add_into(above, far_a, below, far_b)
    whole = lambda v: v.reshape(1, FEAT, HALF)
    above, below = whole(to_x(above, 1)), whole(to_x(below, -1))
    mine, theirs = halves(down_own, above, below)
    (down_grad,) = join(mine, to_core(theirs))
    return (expert_output, token_grad, gate_grad, up_grad, down_grad.T)


def solution(mesh):
    placed = (
        P(("dp", "tensor"), None),
        P(("dp", "tensor"), None),
        P(("dp", "tensor"), None),
        P(("dp", "tensor")),
        P(None, "tensor"),
        P(None, "tensor"),
        P("tensor", None),
    )
    return jax.shard_map(
        local,
        mesh=mesh,
        in_specs=placed,
        out_specs=(
            P(("dp", "tensor"), None),
            P(("dp", "tensor"), None),
            P("dp", "tensor"),
            P("dp", "tensor"),
            P("tensor", "dp"),
        ),
        check_vma=False,
    )
```
